128 devices in a mesh: ctx: 16 (over y_hi, x, core), fsdp: 8 (over z, y_lo).
Axes of the slice: x: 4, y: 4 (y_hi: 2, y_lo: 2; y = y_hi * 2 + y_lo), z: 4, core: 2. Of those that a mesh axis runs over, the one named last changes fastest.
Arguments:
- tokens: bfloat16 [8, 2048, 1280], P('fsdp', 'ctx'), may hold values from -6 to 6
- cotangent: bfloat16 [8, 2048, 1280], P('fsdp', 'ctx'), may hold values from -6 to 6
- lengths: int32 [8, 4], P('fsdp'), may hold values from 1 to 1024, 2048 in all within a row
- block_order: int32 [8, 16], P('fsdp'), may hold values from 0 to 15, each once within a row
- w_query: bfloat16 [1280, 1280], P('fsdp'), may hold values from -0.15625 to 0.15625
- w_key: bfloat16 [1280, 1280], P('fsdp'), may hold values from -0.15625 to 0.15625
- w_value: bfloat16 [1280, 1280], P('fsdp'), may hold values from -0.15625 to 0.15625
- w_out: bfloat16 [1280, 1280], P('fsdp'), may hold values from -1.25 to 1.25
- w_up: bfloat16 [1280, 1280], P('fsdp'), may hold values from -0.15625 to 0.15625
- w_down: bfloat16 [1280, 1280], P('fsdp'), may hold values from -0.15625 to 0.15625
- g_attn: float32 [1280], replicated, may hold values from 0.1 to 1.9
- g_mlp: float32 [1280], replicated, may hold values from 0.1 to 1.9
- q_scale: float32 [80], replicated, may hold values from -1 to 1
- b_up: float32 [1280], replicated, may hold values from -3 to 3
- b_down: float32 [1280], replicated, may hold values from -3 to 3
Outputs:
- layer_out: bfloat16 [8, 2048, 1280], P('fsdp', 'ctx')
- input_grad: float32 [8, 2048, 1280], P('fsdp', 'ctx')
- grad_w_query: float32 [1280, 1280], P(('ctx', 'fsdp'))
- grad_w_key: float32 [1280, 1280], P(('ctx', 'fsdp'))
- grad_w_value: float32 [1280, 1280], P(('ctx', 'fsdp'))
- grad_w_out: float32 [1280, 1280], P(('ctx', 'fsdp'))
- grad_w_up: float32 [1280, 1280], P(('ctx', 'fsdp'))
- grad_w_down: float32 [1280, 1280], P(('ctx', 'fsdp'))
- grad_g_attn: float32 [1280], replicated
- grad_g_mlp: float32 [1280], replicated
- grad_q_scale: float32 [80], replicated
- grad_b_up: float32 [1280], replicated
- grad_b_down: float32 [1280], replicated
The draws below stay inside these ranges and needn't reach their ends.
Inputs may be any that keep to these rules, and one draw needn't show every extreme that they name: Each row holds the 4 lengths of one group's sequences; they sum to 2048 and the longest is exactly 1024. `block_order`: each row is a permutation of the group's 16 block numbers.
All inputs are finite; a program needn't handle non-finite values.
Results may differ from the reference program's by a relative error of at most 0.015.
Values may be sent and summed in bfloat16 or wider, within the bound.
A program may use at most 192 MiB of HBM per device.

```python
import math
from functools import partial
import jax
import jax.numpy as jnp
import numpy as np
from jax import lax

D = 1280
HEADS = 16
HEAD_DIM = 80
FF = 1280
BLK = 128
SEQS = 4
GROUP_TOK = 2048
NBLK = 16
N_FSDP = 8


def level_of(key, dims, split, low, largest):
    level, own = 1.0, jax.random.fold_in(key, 6)
    for axis_at, blocks in split:
        draws = jnp.exp(jax.random.uniform(jax.random.fold_in(own, axis_at), (blocks,), jnp.float32, low / len(split), largest / len(split)))
        level = level * jnp.repeat(draws, dims[axis_at] // blocks).reshape([-1 if axis == axis_at else 1 for axis in range(len(dims))])
    return level


def split_up(number_of, total, bound, lean):
    portions = [(1 << 20) // math.isqrt(rank ** lean) + 1 for rank in range(2, number_of + 1)]
    rest, holding = total - bound - (number_of - 1), [1] * (number_of - 1)
    while rest > 0:
        movable = [i for i in range(number_of - 1) if holding[i] < bound]
        whole, budget = sum([portions[i] for i in movable]), rest
        for i in movable:
            more = min(bound - holding[i], max(1, budget * portions[i] // whole), rest)
            holding[i] = holding[i] + more
            rest = rest - more
    return np.array([bound] + holding)


def uneven_parts(stream_key, amount, total, bound, slope):
    if amount == 2:
        one = jax.random.randint(stream_key, (), max(1, total - bound), min(bound, total - 1) + 1)
        return jnp.stack([one, total - one])
    sizes = jnp.asarray(split_up(amount, total, bound, slope), jnp.int32)
    pairs = (amount - 1) // 2
    source_of, receiver = sizes[1:1 + 2 * pairs:2], sizes[2:2 + 2 * pairs:2]
    slack = jnp.minimum(source_of - 1, bound - receiver)
    moved = jax.random.randint(jax.random.fold_in(stream_key, 1), (pairs,), 0, 1 << 20) % (slack + 1)
    sizes = sizes.at[1:1 + 2 * pairs:2].set(source_of - moved).at[2:2 + 2 * pairs:2].set(receiver + moved)
    return sizes[jax.random.permutation(jax.random.fold_in(stream_key, 2), amount)]


def bell_draw(stream_key, shape, deviation, limit, shards=(), kind=jnp.bfloat16):
    array = deviation * jax.random.normal(stream_key, shape, jnp.float32)
    if shards:
        array = array * level_of(stream_key, shape, shards, -0.22, 0.18)
    return jnp.clip(array, -limit, limit).astype(kind)


def setup_inputs(seed: int = 0) -> dict:
    key_list = jax.random.split(jax.random.key(seed), 16)
    tokens = bell_draw(key_list[0], (N_FSDP, GROUP_TOK, D), 1.0, 6.0, ((0, 8), (1, 16)))
    cotangent = bell_draw(key_list[1], (N_FSDP, GROUP_TOK, D), 1.0, 6.0, ((0, 8), (1, 16)))
    lengths = jax.vmap(lambda own: uneven_parts(own, SEQS, GROUP_TOK, GROUP_TOK // 2, 2))(jax.random.split(key_list[2], N_FSDP)).reshape((N_FSDP, SEQS)).astype(jnp.int32)
    block_order = jax.vmap(lambda own: jax.random.permutation(own, NBLK))(jax.random.split(key_list[3], N_FSDP)).reshape((N_FSDP, NBLK)).astype(jnp.int32)
    w_query = bell_draw(key_list[4], (D, D), D ** -0.5, 0.15625, ((0, 8),))
    w_key = bell_draw(key_list[5], (D, D), D ** -0.5, 0.15625, ((0, 8),))
    w_value = bell_draw(key_list[6], (D, D), D ** -0.5, 0.15625, ((0, 8),))
    w_out = bell_draw(key_list[7], (D, D), (D // 64) ** -0.5, 1.25, ((0, 8),))
    w_up = bell_draw(key_list[8], (D, FF), D ** -0.5, 0.15625, ((0, 8),))
    w_down = bell_draw(key_list[9], (FF, D), FF ** -0.5, 0.15625, ((0, 8),))
    g_attn = jnp.clip(1.0 + 0.18 * jax.random.normal(key_list[10], (D,), jnp.float32), 0.1, 1.9)
    g_mlp = jnp.clip(1.0 + 0.18 * jax.random.normal(key_list[11], (D,), jnp.float32), 0.1, 1.9)
    q_scale = jnp.clip(jax.random.uniform(key_list[12], (HEAD_DIM,), jnp.float32, -1.0, 1.0), -1.0, 1.0)
    b_up = bell_draw(key_list[13], (FF,), 0.5, 3.0, (), jnp.float32)
    b_down = bell_draw(key_list[14], (D,), 0.5, 3.0, (), jnp.float32)
    return {"tokens": tokens, "cotangent": cotangent, "lengths": lengths, "block_order": block_order, "w_query": w_query, "w_key": w_key, "w_value": w_value, "w_out": w_out, "w_up": w_up, "w_down": w_down, "g_attn": g_attn, "g_mlp": g_mlp, "q_scale": q_scale, "b_up": b_up, "b_down": b_down}


epsilon = 1e-06
query_const = 1.442695
masked_score = -1e+30
highest = lax.Precision.HIGHEST

@jax.custom_vjp
def low(v):
    return lax.optimization_barrier(v.astype(jnp.bfloat16)).astype(jnp.float32)

@jax.custom_vjp
def low_back(v):
    return v

def low_keep(v):
    return (low(v), None)

def low_pass(kept, grad):
    return (grad,)

def back_keep(v):
    return (v, None)

def back_low(kept, grad):
    return (low(grad),)
low.defvjp(low_keep, low_pass)
low_back.defvjp(back_keep, back_low)

def matmul(first_op, second_op):
    return jnp.dot(first_op, second_op, precision=highest)

def rms_norm(values):
    return values * lax.rsqrt(lax.optimization_barrier(jnp.mean(values * values, axis=-1, keepdims=True)) + epsilon)

def places(lengths_row, order_row):
    slot_ids = jnp.arange(GROUP_TOK, dtype=jnp.int32)
    position = order_row[slot_ids // BLK] * BLK + slot_ids % BLK
    seq_ends = jnp.cumsum(lengths_row)
    seq_ids = lax.optimization_barrier(jnp.sum((position[:, None] >= seq_ends[None, :]).astype(jnp.int32), axis=1))
    return (position, seq_ids)

def attend_head(allowed, head_item):
    query_h, keys_h, values_h = head_item
    scores = low_back(jnp.dot(query_h, keys_h.T, precision=highest))
    scores = jnp.where(allowed, scores, masked_score)
    row_max = lax.optimization_barrier(jnp.max(scores, axis=1, keepdims=True))
    exp_scores = jnp.exp(scores - row_max)
    probabilities = exp_scores / lax.optimization_barrier(jnp.sum(exp_scores, axis=1, keepdims=True))
    return matmul(low(probabilities), values_h)

def split_heads(matrix):
    return matrix.reshape(GROUP_TOK, HEADS, HEAD_DIM).transpose(1, 0, 2)

def forward(x_in, w_query, w_key, w_value, w_out, w_up, w_down, g_attn, g_mlp, q_scale, b_up, b_down, allowed):
    normed = low(rms_norm(x_in) * g_attn)
    scale_vec = query_const / math.sqrt(HEAD_DIM) * jax.nn.softplus(q_scale)
    queries = low(low_back(matmul(normed, w_query)).reshape(GROUP_TOK, HEADS, HEAD_DIM) * scale_vec)
    key_rows = low(low_back(matmul(normed, w_key)))
    value_rows = low(low_back(matmul(normed, w_value)))
    per_head = lax.map(jax.checkpoint(partial(attend_head, allowed)), (queries.transpose(1, 0, 2), split_heads(key_rows), split_heads(value_rows)))
    mixed_heads = low(low_back(per_head.transpose(1, 0, 2).reshape(GROUP_TOK, HEADS * HEAD_DIM)))
    after_attn = x_in + low_back(matmul(mixed_heads, w_out))
    normed_two = low(rms_norm(after_attn) * g_mlp)
    hidden = low_back(matmul(normed_two, w_up) + b_up)
    active = low(jax.nn.silu(hidden))
    return after_attn + matmul(active, w_down) + b_down

def reference(tokens, cotangent, lengths, block_order, w_query, w_key, w_value, w_out, w_up, w_down, g_attn, g_mlp, q_scale, b_up, b_down):
    params = tuple((weight.astype(jnp.float32) for weight in (w_query, w_key, w_value, w_out, w_up, w_down, g_attn, g_mlp, q_scale, b_up, b_down)))

    def one_group(running, group_item):
        tokens_g, cot_g, lengths_g, order_g = group_item
        position, seq_ids = places(lengths_g, order_g)
        allowed = (seq_ids[:, None] == seq_ids[None, :]) & (position[None, :] <= position[:, None])

        def one_layer(x_in, *weights):
            return forward(x_in, *weights, allowed)
        output, pullback = jax.vjp(one_layer, tokens_g.astype(jnp.float32), *params)
        gradients = pullback(cot_g.astype(jnp.float32))
        summed = tuple((prior + gradient for prior, gradient in zip(running, gradients[1:])))
        return (summed, (output.astype(jnp.bfloat16), gradients[0]))
    zero_sums = tuple((jnp.zeros_like(weight) for weight in params))
    weight_sums, (layer_out, input_grad) = lax.scan(one_group, zero_sums, (tokens, cotangent, lengths, block_order))
    return (layer_out, input_grad, weight_sums[0], weight_sums[1], weight_sums[2], weight_sums[3], weight_sums[4], weight_sums[5], weight_sums[6], weight_sums[7], weight_sums[8], weight_sums[9], weight_sums[10])
```

```python
import functools
import math

import jax
import jax.numpy as jnp
from jax import lax
from jax.experimental import pallas as pl
from jax.experimental.pallas import tpu as pltpu
from jax.sharding import PartitionSpec as P

D = 1280
HEADS = 16
HEAD_DIM = 80
BLK = 128
GROUP = 2048
NBLK = 16
SHARD = 160
HALF = 640
TILE = 256
WINDOW = 1024
EPS = 1e-06
QUERY_CONST = 1.442695 / math.sqrt(HEAD_DIM)
MASKED = -1e30
N_SEM = 256
MESH = pl.DeviceIdType.MESH
bf16, f32 = jnp.bfloat16, jnp.float32


def nn(a, b):
    return jnp.dot(a, b, preferred_element_type=f32)


def nt(a, b):
    return lax.dot_general(a, b, (((1,), (1,)), ((), ())), preferred_element_type=f32)


def ds(start, size, unit):
    return pl.ds(pl.multiple_of(start, unit), size)


def flip(matrix):
    return matrix.astype(f32).T.astype(matrix.dtype)


class Wire:
    def __init__(self, send_sems, recv_sems):
        self.send_sems, self.recv_sems, self.used, self.sent = send_sems, recv_sems, 0, []

    def copy(self, index, src, dst, device):
        return pltpu.make_async_remote_copy(
            src_ref=src, dst_ref=dst, send_sem=self.send_sems.at[index], recv_sem=self.recv_sems.at[index],
            device_id=device, device_id_type=MESH,
        )

    def send(self, src, dst, device):
        index = self.used
        self.used += 1
        copy = self.copy(index, src, dst, device)
        copy.start()
        self.sent.append(copy)
        return index

    def receive(self, index, ref, device):
        self.copy(index, ref, ref, device).wait_recv()

    def drain(self):
        for copy in self.sent:
            copy.wait_send()
        self.sent = []


def layer(
    lengths, order, tokens, cot, wqkv, w_out, w_up, w_down, w_query, w_key, w_value,
    g_attn, g_mlp, q_scale, b_up, b_down,
    layer_out, input_grad, grad_mlp, grad_qkv, small_out,
    later_weights,
    weights, gathered, wqkv_all, wqkv_t, raw_q, qkv_slot, qkv_pos, raw_pos, k_rows, v_rows, probs, out_pos,
    head_send, mixed_t, dout_t, dout_slot, dout_pos, dk_acc, dv_acc, grads_pos, grads_flat, grads_in,
    acts, up_in, up_all, t1, r1, t2, r2, t3, r3, swap_out, rows_out, rows_in,
    gw, gw_send, gw_in, gq_send, gq_in, ar_own, ar_one, ar_mid, ar_two,
    local_sems, send_sems, recv_sems,
):
    c, f = lax.axis_index("ctx"), lax.axis_index("fsdp")
    y_hi, x, core = c // 8, (c // 2) % 4, c % 2
    z, y_lo = f // 2, f % 2
    y = 2 * y_hi + y_lo

    def at(x_at, y_at, z_at, core_at):
        return ((y_at // 2) * 8 + x_at * 2 + core_at, z_at * 2 + y_at % 2)

    def away(dx=0, dy=0, dz=0):
        return at((x + dx) % 4, (y + dy) % 4, (z + dz) % 4, core)

    sibling = (c + 1 - 2 * core, f)
    wire = Wire(send_sems, recv_sems)

    axes = {0: "xzy", 1: "yxz", 2: "zyx"}
    here = {"x": x, "y": y, "z": z}

    def final_target(w):
        a, b, last = (here[n] for n in axes[w])
        return (4 * a + b, 2 * last + core)

    def final_source(w):
        found = dict(zip(axes[w], (c // 4, c % 4, f // 2)))
        return at(found["x"], found["y"], found["z"], f % 2)

    own_rows = ds(f * SHARD, SHARD, SHARD)
    loads = []
    for j, ref in enumerate((w_out, w_up, w_down, w_query, w_key, w_value)):
        load = pltpu.make_async_copy(ref, (weights, later_weights)[j // 3].at[j % 3, own_rows], local_sems.at[j])
        load.start()
        loads.append(load)

    barrier = pltpu.get_barrier_semaphore()
    peers = [((c + k) % 16, f) for k in range(1, 16)] + [(c, (f + k) % 8) for k in range(1, 8)]
    peers.append(at(x, 3 - y, z, core))
    for w in range(3):
        peers += [final_target(w), final_source(w)]
    for peer in peers:
        pl.semaphore_signal(barrier, inc=1, device_id=peer, device_id_type=MESH)

    x_in = tokens[...].astype(f32)
    r_one = lax.rsqrt(jnp.mean(x_in * x_in, axis=1, keepdims=True) + EPS)
    gathered[ds(c * BLK, BLK, BLK), :] = (x_in * r_one * g_attn[...]).astype(bf16)
    wqkv_all[own_rows, :] = wqkv[...]
    scale = QUERY_CONST * jnp.log(1.0 + jnp.exp(q_scale[...]))
    scale_col = jnp.broadcast_to(scale, (BLK, HEAD_DIM)).T[:, :1]

    pl.semaphore_wait(barrier, len(peers))

    def piece(yh, xa, co, part=None):
        start = ((yh * 4 + xa) * 2 + co) * BLK
        if part is None:
            return gathered.at[ds(start, BLK, BLK)]
        return gathered.at[ds(start + part * 64, 64, 64)]

    other = 1 - y_hi
    xl, xr, xo = (x + 3) % 4, (x + 1) % 4, (x + 2) % 4
    own = piece(y_hi, x, core)
    to_y = wire.send(own, own, away(dy=2))
    to_xr = wire.send(own, own, away(dx=1))
    to_xl = wire.send(own, own, away(dx=3))
    to_core = wire.send(own, own, sibling)
    cols = []
    for k in range(1, 8):
        cols.append(wire.send(wqkv_all.at[own_rows], wqkv_all.at[own_rows], (c, (f + k) % 8)))

    half_cols = ds(core * HALF, HALF, 128)
    across_y = (y + 1 + 2 * core) % 4
    from_y = (y + 3 + 2 * core) % 4

    def rows_of(buffer, zz, lo, part=None):
        start = (zz * 2 + lo) * SHARD
        if part is None:
            return buffer.at[:, ds(start, SHARD, SHARD), half_cols]
        return buffer.at[:, ds(start + part * 80, 80, 80), half_cols]

    zl, zr, zo = (z + 3) % 4, (z + 1) % 4, (z + 2) % 4

    class Gather:
        def __init__(self, buffer, own):
            self.buffer, self.own = buffer, own

        def begin(self):
            one = rows_of(self.buffer, z, y_lo)
            for load in self.own:
                load.wait()
            self.y = wire.send(one, one, at(x, across_y, z, core))
            self.r0 = wire.send(one, one, away(dz=1))
            self.l0 = wire.send(one, one, away(dz=3))
            self.kept = []

        def give(self, ref):
            self.kept.append((wire.send(ref, ref, sibling), ref))

        def second(self):
            two = rows_of(self.buffer, z, 1 - y_lo)
            wire.receive(self.y, two, at(x, from_y, z, core))
            self.r1 = wire.send(two, two, away(dz=1))
            self.l1 = wire.send(two, two, away(dz=3))
            self.give(two)

        def forward(self, lo, left, right):
            a, b = rows_of(self.buffer, zl, lo), rows_of(self.buffer, zr, lo)
            wire.receive(right, a, away(dz=3))
            ah = rows_of(self.buffer, zl, lo, 0)
            ka = wire.send(ah, ah, away(dz=1))
            self.give(a)
            wire.receive(left, b, away(dz=1))
            bh = rows_of(self.buffer, zr, lo, 1)
            kb = wire.send(bh, bh, away(dz=3))
            self.give(b)
            return ka, kb

        def third(self):
            self.f0 = self.forward(y_lo, self.l0, self.r0)

        def fourth(self):
            self.f1 = self.forward(1 - y_lo, self.l1, self.r1)

        def last(self, lo, pair):
            wire.receive(pair[0], rows_of(self.buffer, zo, lo, 0), away(dz=3))
            wire.receive(pair[1], rows_of(self.buffer, zo, lo, 1), away(dz=1))
            self.give(rows_of(self.buffer, zo, lo))

        def fifth(self):
            self.last(y_lo, self.f0)

        def sixth(self):
            self.last(1 - y_lo, self.f1)

        def finish(self):
            for index, ref in self.kept:
                wire.receive(index, ref, sibling)

    first_set, second_set = Gather(weights, loads[:3]), Gather(later_weights, loads[3:])
    first_set.begin()

    def project(yh, xa):
        chip = yh * 4 + xa
        both = nt(wqkv_t[...], gathered[ds(chip * TILE, TILE, TILE), :])
        for i in range(2):
            one = both[:, i * BLK:(i + 1) * BLK]
            raw_q[2 * chip + i] = one[:HEAD_DIM]
            qkv_slot[2 * chip + i, :HEAD_DIM] = (one[:HEAD_DIM] * scale_col).astype(bf16)
            qkv_slot[2 * chip + i, HEAD_DIM:] = one[HEAD_DIM:240].astype(bf16)

    for k, index in enumerate(cols):
        src_f = (f + 7 - k) % 8
        wire.receive(index, wqkv_all.at[ds(src_f * SHARD, SHARD, SHARD)], (c, src_f))
    wqkv_t[...] = flip(wqkv_all[...])

    def pass_on(index, ref, device):
        wire.receive(index, ref, device)
        return wire.send(ref, ref, sibling)

    wire.receive(to_core, piece(y_hi, x, 1 - core), sibling)
    project(y_hi, x)
    core_l = pass_on(to_xr, piece(y_hi, xl, core), away(dx=3))
    ring_r = wire.send(piece(y_hi, xl, core, 0), piece(y_hi, xl, core, 0), away(dx=1))
    core_r = pass_on(to_xl, piece(y_hi, xr, core), away(dx=1))
    ring_l = wire.send(piece(y_hi, xr, core, 1), piece(y_hi, xr, core, 1), away(dx=3))
    core_y = pass_on(to_y, piece(other, x, core), away(dy=2))
    y_r = wire.send(piece(other, x, core), piece(other, x, core), away(dx=1))
    y_l = wire.send(piece(other, x, core), piece(other, x, core), away(dx=3))
    first_set.second()
    wire.receive(core_l, piece(y_hi, xl, 1 - core), sibling)
    project(y_hi, xl)
    wire.receive(core_r, piece(y_hi, xr, 1 - core), sibling)
    project(y_hi, xr)
    wire.receive(core_y, piece(other, x, 1 - core), sibling)
    project(other, x)
    wire.receive(ring_r, piece(y_hi, xo, core, 0), away(dx=3))
    wire.receive(ring_l, piece(y_hi, xo, core, 1), away(dx=1))
    far = wire.send(piece(y_hi, xo, core), piece(y_hi, xo, core), away(dy=2))
    core_o = wire.send(piece(y_hi, xo, core), piece(y_hi, xo, core), sibling)
    core_yl = pass_on(y_r, piece(other, xl, core), away(dx=3))
    core_yr = pass_on(y_l, piece(other, xr, core), away(dx=1))
    first_set.third()
    wire.receive(core_o, piece(y_hi, xo, 1 - core), sibling)
    project(y_hi, xo)
    wire.receive(core_yl, piece(other, xl, 1 - core), sibling)
    project(other, xl)
    wire.receive(core_yr, piece(other, xr, 1 - core), sibling)
    project(other, xr)
    core_f = pass_on(far, piece(other, xo, core), away(dy=2))
    wire.receive(core_f, piece(other, xo, 1 - core), sibling)
    project(other, xo)

    slot_of = []
    for p in range(NBLK):
        slot = 0
        for b in range(NBLK):
            slot = jnp.where(order[0, b] == p, b, slot)
        slot_of.append(slot)
    for p in range(NBLK):
        qkv_pos[:, p * BLK:(p + 1) * BLK] = qkv_slot[slot_of[p]]
        raw_pos[:, p * BLK:(p + 1) * BLK] = raw_q[slot_of[p]]
    k_rows[...] = flip(qkv_pos[HEAD_DIM:2 * HEAD_DIM, :])
    v_rows[...] = flip(qkv_pos[2 * HEAD_DIM:, :])

    ends, total = [], 0
    for s in range(4):
        total = total + lengths[0, s]
        ends.append(total)

    at_part = 0
    parts_of = []
    for t in range(GROUP // TILE):
        low, high = max(0, t * TILE - WINDOW), (t + 1) * TILE
        width = high - low
        tile = slice(t * TILE, high)
        scores = nn(k_rows[low:high, :], qkv_pos[:HEAD_DIM, tile])
        at_q = t * TILE + lax.broadcasted_iota(jnp.int32, (1, TILE), 1)
        start = jnp.zeros((1, TILE), jnp.int32)
        for end in ends:
            start = jnp.where(at_q >= end, end, start)
        at_k = low + lax.broadcasted_iota(jnp.int32, (width, TILE), 0)
        scores = jnp.where((at_k <= at_q) & (at_k >= start), scores, MASKED)
        top = jnp.max(scores, axis=0, keepdims=True)
        powers = jnp.exp(scores - top)
        part = powers * (1.0 / jnp.sum(powers, axis=0, keepdims=True))
        part = part.astype(bf16)
        parts_of.append(slice(at_part, at_part + width))
        at_part += width
        probs[parts_of[t], :] = part
        out = nn(qkv_pos[2 * HEAD_DIM:, low:high], part).astype(bf16)
        out_pos[2 * t] = out[:, :BLK]
        out_pos[2 * t + 1] = out[:, BLK:]

    for b in range(NBLK):
        head_send[b] = out_pos[order[0, b]]

    def exchange(src_of, dst):
        return [wire.send(src_of((c + k) % 16), dst, ((c + k) % 16, f)) for k in range(1, 16)]

    def arrive(indices, dst_of):
        for k, index in enumerate(indices):
            src = (c + 15 - k) % 16
            wire.receive(index, dst_of(src), (src, f))

    head_rows = ds(c * HEAD_DIM, HEAD_DIM, HEAD_DIM)
    mixing = exchange(lambda b: head_send.at[b], mixed_t.at[head_rows])
    mixed_t[head_rows, :] = head_send[c]
    first_set.fourth()
    first_set.fifth()
    first_set.sixth()
    first_set.finish()
    wire.set_one = len(wire.sent)
    second_set.begin()

    cot_f = cot[...].astype(f32)

    def spread(a, w):
        return jnp.concatenate([nn(a, weights[w, :, n:n + 256]) for n in range(0, D, 256)], axis=1)

    def spread_back(a, w):
        return jnp.concatenate([nt(a, weights[w, n:n + 256, :]) for n in range(0, D, 256)], axis=1)

    grad_active = spread_back(cot[...], 2)
    arrive(mixing, lambda src: mixed_t.at[ds(src * HEAD_DIM, HEAD_DIM, HEAD_DIM)])

    mixed = flip(mixed_t[...])
    after = x_in + spread(mixed, 0)
    r_two = lax.rsqrt(jnp.mean(after * after, axis=1, keepdims=True) + EPS)
    n_two = after * r_two
    normed_two = (n_two * g_mlp[...]).astype(bf16)
    hidden = spread(normed_two, 1) + b_up[...]
    gate = jax.nn.sigmoid(hidden)
    active = (hidden * gate).astype(bf16)
    grad_hidden = (grad_active * gate * (1.0 + hidden * (1.0 - gate))).astype(bf16)
    back_two = spread_back(grad_hidden, 1)
    scaled = back_two * g_mlp[...]
    grad_after = cot_f + r_two * (scaled - n_two * jnp.mean(scaled * n_two, axis=1, keepdims=True))
    grad_branch = grad_after.astype(bf16)
    dout_t[...] = flip(spread_back(grad_branch, 0).astype(bf16))
    douts = exchange(lambda b: dout_t.at[ds(b * HEAD_DIM, HEAD_DIM, HEAD_DIM)], dout_slot.at[c])
    dout_slot[c] = dout_t[head_rows, :]

    my_lanes = ds(core * BLK, BLK, BLK)
    other_half = ds((1 - core) * HALF, HALF, 128)
    ups = (grad_branch, grad_hidden, cot[...])
    acts[0, :, my_lanes] = mixed_t[...]
    acts[1, :, my_lanes] = flip(normed_two)
    acts[2, :, my_lanes] = flip(active)
    for w in range(3):
        up_in[w] = ups[w]
    give_acts = wire.send(acts.at[:, :, my_lanes], acts.at[:, :, my_lanes], sibling)
    give_up = wire.send(up_in.at[:, :, other_half], up_all.at[:, my_lanes], sibling)
    for w in range(3):
        up_all[w, my_lanes, :] = up_in[w, :, half_cols]
    layer_out[...] = (after + spread(active, 2) + b_down[...]).astype(bf16)
    input_grad[...] = grad_after
    ar_own[...] = jnp.zeros_like(ar_own)
    ar_own[1:2, :] = jnp.sum(back_two * n_two, axis=0, keepdims=True)
    ar_own[2:3, :] = jnp.sum(grad_hidden.astype(f32), axis=0, keepdims=True)
    ar_own[3:4, :] = jnp.sum(cot_f, axis=0, keepdims=True)

    second_set.second()
    sib_lanes = ds((1 - core) * BLK, BLK, BLK)
    wire.receive(give_acts, acts.at[:, :, sib_lanes], sibling)
    wire.receive(give_up, up_all.at[:, sib_lanes], sibling)

    def scatter(w, stage, src_of, dst_of):
        axis = axes[w][stage]
        return [
            wire.send(src_of((here[axis] + k) % 4), dst_of(k - 1), away(**{"d" + axis: k})) for k in range(1, 4)
        ]

    def gathered_sum(w, stage, indices, first, buffers):
        axis = axes[w][stage]
        for k, index in enumerate(indices):
            wire.receive(index, buffers.at[w, k], away(**{"d" + axis: 3 - k}))
        return first.astype(f32) + buffers[w, 0].astype(f32) + buffers[w, 1].astype(f32) + buffers[w, 2].astype(f32)

    stage_one, stage_two, stage_three = {}, {}, {}
    for w in (2, 1, 0):
        for n in range(0, D, 320):
            rows = slice(n, n + 320)
            t1[w, rows, :] = nn(acts[w, rows, :], up_all[w]).astype(bf16)
        stage_one[w] = scatter(w, 0, lambda d: t1.at[w, ds(d * 320, 320, 320)], lambda k: r1.at[w, k])

    def second_stage(w):
        mine = t1[w, ds(here[axes[w][0]] * 320, 320, 320), :]
        t2[w] = gathered_sum(w, 0, stage_one[w], mine, r1).astype(bf16)
        stage_two[w] = scatter(w, 1, lambda d: t2.at[w, ds(d * 80, 80, 80)], lambda k: r2.at[w, k])

    def third_stage(w):
        mine = t2[w, ds(here[axes[w][1]] * 80, 80, 80), :]
        both = gathered_sum(w, 1, stage_two[w], mine, r2)
        for d in range(4):
            t3[w, d] = jnp.concatenate([both[20 * d:20 * d + 20], jnp.zeros((12, HALF), f32)], axis=0).astype(bf16)
        stage_three[w] = scatter(w, 2, lambda d: t3.at[w, d], lambda k: r3.at[w, k])

    def fourth_stage(w):
        both = gathered_sum(w, 2, stage_three[w], t3[w, here[axes[w][2]]], r3)
        for i in range(2):
            swap_out[w, i] = jnp.concatenate([both[10 * i:10 * i + 10], jnp.zeros((6, HALF), f32)], axis=0)
        rows_out[w, :, half_cols] = swap_out[w, core]
        return wire.send(swap_out.at[w, 1 - core], rows_out.at[w, :, half_cols], sibling)

    arrive(douts, lambda src: dout_slot.at[src])

    for p in range(NBLK):
        dout_pos[:, p * BLK:(p + 1) * BLK] = dout_slot[slot_of[p]]
    dk_acc[...] = jnp.zeros_like(dk_acc)
    dv_acc[...] = jnp.zeros_like(dv_acc)
    scale_terms = jnp.zeros((HEAD_DIM, 1), f32)
    for t in range(GROUP // TILE):
        low, high = max(0, t * TILE - WINDOW), (t + 1) * TILE
        width = high - low
        tile = slice(t * TILE, high)
        d_out = dout_pos[:, tile]
        delta = jnp.sum(d_out.astype(f32) * jnp.concatenate([out_pos[2 * t], out_pos[2 * t + 1]], axis=1).astype(f32), axis=0, keepdims=True)
        part = probs[parts_of[t], :]
        d_probs = nn(v_rows[low:high, :], d_out)
        d_scores = (part.astype(f32) * (d_probs - delta)).astype(bf16)
        dq = nn(qkv_pos[HEAD_DIM:2 * HEAD_DIM, low:high], d_scores)
        scale_terms = scale_terms + jnp.sum(dq * raw_pos[:, tile], axis=1, keepdims=True)
        dq = (dq * scale_col).astype(bf16)
        grads_pos[2 * t, :HEAD_DIM] = dq[:, :BLK]
        grads_pos[2 * t + 1, :HEAD_DIM] = dq[:, BLK:]
        dk_acc[:, low:high] += nt(qkv_pos[:HEAD_DIM, tile], d_scores)
        dv_acc[:, low:high] += nt(d_out, part)

    for p in range(NBLK):
        lanes = slice(p * BLK, (p + 1) * BLK)
        grads_pos[p, HEAD_DIM:2 * HEAD_DIM] = dk_acc[:, lanes].astype(bf16)
        grads_pos[p, 2 * HEAD_DIM:] = dv_acc[:, lanes].astype(bf16)
    for b in range(NBLK):
        block = grads_pos[order[0, b]]
        qkv_slot[b] = block
        grads_flat[:, b * BLK:(b + 1) * BLK] = block
    sent_grads = exchange(lambda b: qkv_slot.at[b], grads_in.at[c])
    grads_in[c] = qkv_slot[c]

    second_set.third()
    second_set.fourth()

    for n in range(0, D, 256):
        grad_t = nn(grads_flat[...], gathered[:, n:n + 256])
        gw[n:n + 256, :] = jnp.concatenate([grad_t, jnp.zeros((16, 256), f32)], axis=0).T
    for fs in range(8):
        picked = [gw[cs * 80 + fs * 10:cs * 80 + fs * 10 + 10, :] for cs in range(16)]
        gw_send[fs] = jnp.concatenate(picked, axis=0).astype(bf16)
    shares = [wire.send(gw_send.at[(f + k) % 8], gw_in.at[k - 1], (c, (f + k) % 8)) for k in range(1, 8)]

    for w in (2, 1, 0):
        second_stage(w)
    second_set.fifth()
    second_set.sixth()
    second_set.finish()
    for w in (2, 1, 0):
        third_stage(w)

    for copy in wire.sent[:wire.set_one]:
        copy.wait_send()
    wire.sent = wire.sent[wire.set_one:]
    loads = []
    for j in range(3):
        load = pltpu.make_async_copy(later_weights.at[j], weights.at[j], local_sems.at[j])
        load.start()
        loads.append(load)
    arrive(sent_grads, lambda src: grads_in.at[src])
    grad_normed = jnp.zeros((BLK, D), f32)
    for j in range(3):
        loads[j].wait()
        rows = slice(j * HEAD_DIM, (j + 1) * HEAD_DIM)
        joined = jnp.concatenate([grads_in[h, rows] for h in range(HEADS)], axis=0)
        grad_normed = grad_normed + spread_back(flip(joined), j)
    n_one = x_in * r_one
    scaled = grad_normed * g_attn[...]
    through = r_one * (scaled - n_one * jnp.mean(scaled * n_one, axis=1, keepdims=True))
    input_grad[...] = input_grad[...] + through
    ar_own[0:1, :] = jnp.sum(grad_normed * n_one, axis=0, keepdims=True)
    ar_own[4:5, :HEAD_DIM] = jnp.broadcast_to(scale_terms, (HEAD_DIM, BLK)).T[:1]
    ar_one[c] = ar_own[...]
    sums = exchange(lambda b: ar_own, ar_one.at[c])

    swaps = [(w, fourth_stage(w)) for w in (2, 1, 0)]
    for k, index in enumerate(shares):
        src_f = (f + 7 - k) % 8
        wire.receive(index, gw_in.at[k], (c, src_f))
    both = gw_send[f].astype(f32)
    for k in range(7):
        both = both + gw_in[k].astype(f32)
    for cs in range(16):
        gq_send[cs] = jnp.concatenate([both[10 * cs:10 * cs + 10], jnp.zeros((6, 256), f32)], axis=0).astype(bf16)
    gq_in[c] = gq_send[c]
    heads = exchange(lambda b: gq_send.at[b], gq_in.at[c])

    finals = []
    for w, index in swaps:
        wire.receive(index, rows_out.at[w, :, other_half], sibling)
        target = final_target(w)
        index = wire.used
        wire.used += 1
        stays = (target[0] == c) & (target[1] == f)
        copy = wire.copy(index, rows_out.at[w], rows_in.at[w], target)
        within = pltpu.make_async_copy(rows_out.at[w], rows_in.at[w], recv_sems.at[index])
        pl.when(jnp.logical_not(stays))(copy.start)
        pl.when(stays)(within.start)
        finals.append((w, index, copy, stays))

    arrive(sums, lambda src: ar_one.at[src])
    total_small = ar_one[0]
    for k in range(1, 16):
        total_small = total_small + ar_one[k]
    ar_mid[...] = total_small
    ar_two[f] = total_small
    sums = [wire.send(ar_mid, ar_two.at[f], (c, (f + k) % 8)) for k in range(1, 8)]
    for k, index in enumerate(sums):
        src_f = (f + 7 - k) % 8
        wire.receive(index, ar_two.at[src_f], (c, src_f))
    total_small = ar_two[0]
    for k in range(1, 8):
        total_small = total_small + ar_two[k]
    small_out[...] = total_small

    arrive(heads, lambda src: gq_in.at[src])
    grad_qkv[...] = gq_in[...]
    for w, index, copy, stays in finals:
        wire.receive(index, rows_in.at[w], final_source(w))
        pl.when(jnp.logical_not(stays))(copy.wait_send)
    grad_mlp[...] = rows_in[...]
    wire.drain()
    assert wire.used <= N_SEM


def on_device(
    tokens, cotangent, lengths, block_order, w_query, w_key, w_value, w_out, w_up, w_down,
    g_attn, g_mlp, q_scale, b_up, b_down,
):
    first = lax.axis_index("ctx") * HEAD_DIM
    columns = [lax.dynamic_slice(w, (0, first), (SHARD, HEAD_DIM)) for w in (w_query, w_key, w_value)]
    wqkv = jnp.concatenate(columns + [jnp.zeros((SHARD, 16), bf16)], axis=1)
    vmem, smem, any_space = (pl.BlockSpec(memory_space=s) for s in (pltpu.VMEM, pltpu.SMEM, pl.ANY))
    shapes = {
        "weights": ((3, D, D), bf16), "gathered": ((GROUP, D), bf16), "wqkv_all": ((D, 256), bf16),
        "wqkv_t": ((256, D), bf16), "raw_q": ((NBLK, HEAD_DIM, BLK), f32), "qkv_slot": ((NBLK, 240, BLK), bf16),
        "qkv_pos": ((240, GROUP), bf16), "raw_pos": ((HEAD_DIM, GROUP), f32), "k_rows": ((GROUP, HEAD_DIM), bf16),
        "v_rows": ((GROUP, HEAD_DIM), bf16), "probs": ((7680, TILE), bf16), "out_pos": ((NBLK, HEAD_DIM, BLK), bf16),
        "head_send": ((NBLK, HEAD_DIM, BLK), bf16), "mixed_t": ((D, BLK), bf16), "dout_t": ((D, BLK), bf16),
        "dout_slot": ((NBLK, HEAD_DIM, BLK), bf16), "dout_pos": ((HEAD_DIM, GROUP), bf16),
        "dk_acc": ((HEAD_DIM, GROUP), f32), "dv_acc": ((HEAD_DIM, GROUP), f32), "grads_pos": ((NBLK, 240, BLK), bf16),
        "grads_flat": ((240, GROUP), bf16), "grads_in": ((NBLK, 240, BLK), bf16),
        "acts": ((3, D, 2 * BLK), bf16), "up_in": ((3, BLK, D), bf16), "up_all": ((3, 2 * BLK, HALF), bf16),
        "t1": ((3, D, HALF), bf16), "r1": ((3, 3, 320, HALF), bf16), "t2": ((3, 320, HALF), bf16),
        "r2": ((3, 3, 80, HALF), bf16), "t3": ((3, 4, 32, HALF), bf16), "r3": ((3, 3, 32, HALF), bf16),
        "swap_out": ((3, 2, 16, HALF), f32), "rows_out": ((3, 16, D), f32), "rows_in": ((3, 16, D), f32),
        "gw": ((D, 256), f32), "gw_send": ((8, SHARD, 256), bf16), "gw_in": ((7, SHARD, 256), bf16),
        "gq_send": ((16, 16, 256), bf16), "gq_in": ((16, 16, 256), bf16),
        "ar_own": ((8, D), f32), "ar_one": ((16, 8, D), f32), "ar_mid": ((8, D), f32), "ar_two": ((8, 8, D), f32),
    }
    outs = {
        "layer_out": ((BLK, D), bf16), "input_grad": ((BLK, D), f32), "grad_mlp": ((3, 16, D), f32),
        "grad_qkv": ((16, 16, 256), bf16), "small_out": ((8, D), f32), "later_weights": ((3, D, D), bf16),
    }
    ins = (
        "lengths", "order", "tokens", "cot", "wqkv", "w_out", "w_up", "w_down", "w_query", "w_key", "w_value",
        "g_attn", "g_mlp", "q_scale", "b_up", "b_down",
    )

    def body(*refs):
        names = ins + tuple(outs) + tuple(shapes) + ("local_sems", "send_sems", "recv_sems")
        layer(**dict(zip(names, refs, strict=True)))

    row = lambda v: v.reshape(1, -1)
    out, in_grad, rows, qkv, small, _ = pl.pallas_call(
        body,
        out_shape=[jax.ShapeDtypeStruct(*s) for s in outs.values()],
        in_specs=[smem, smem] + [vmem] * 3 + [any_space] * 6 + [vmem] * 5,
        out_specs=[vmem] * (len(outs) - 1) + [any_space],
        scratch_shapes=[pltpu.VMEM(*s) for s in shapes.values()]
        + [pltpu.SemaphoreType.DMA((6,)), pltpu.SemaphoreType.DMA((N_SEM,)), pltpu.SemaphoreType.DMA((N_SEM,))],
        compiler_params=pltpu.CompilerParams(
            collective_id=0, has_side_effects=True, vmem_limit_bytes=62 << 20
        ),
    )(
        lengths, block_order, tokens[0], cotangent[0], wqkv, w_out, w_up, w_down, w_query, w_key, w_value,
        row(g_attn), row(g_mlp), row(q_scale), row(b_up), row(b_down),
    )
    heads = qkv[:, :10, :240].reshape(16, 10, 3, HEAD_DIM).astype(f32).transpose(2, 1, 0, 3).reshape(3, 10, D)
    grad_scale = small[4, :HEAD_DIM] * QUERY_CONST * jax.nn.sigmoid(q_scale)
    return (
        out[None], in_grad[None], heads[0], heads[1], heads[2], rows[0, :10], rows[1, :10], rows[2, :10],
        small[0], small[1], grad_scale, small[2], small[3],
    )


def solution(mesh):
    tokens, rows, whole = P("fsdp", "ctx", None), P("fsdp", None), P()
    owned = P(("ctx", "fsdp"), None)
    return jax.shard_map(
        on_device, mesh=mesh,
        in_specs=(tokens, tokens, rows, rows) + (rows,) * 6 + (whole,) * 5,
        out_specs=(tokens, tokens) + (owned,) * 6 + (whole,) * 5,
        check_vma=False,
    )
```

```python
import functools
import math

import jax
import jax.numpy as jnp
from jax import lax
from jax.experimental import pallas as pl
from jax.experimental.pallas import tpu as pltpu
from jax.sharding import PartitionSpec as P

D = 1280
HEADS = 16
HEAD_DIM = 80
BLK = 128
GROUP = 2048
NBLK = 16
SHARD = 160
HALF = 640
TILE = 256
WINDOW = 1024
EPS = 1e-06
QUERY_CONST = 1.442695 / math.sqrt(HEAD_DIM)
MASKED = -1e30
N_SEM = 256
MESH = pl.DeviceIdType.MESH
bf16, f32 = jnp.bfloat16, jnp.float32


def nn(a, b):
    return jnp.dot(a, b, preferred_element_type=f32)


def nt(a, b):
    return lax.dot_general(a, b, (((1,), (1,)), ((), ())), preferred_element_type=f32)


def ds(start, size, unit):
    return pl.ds(pl.multiple_of(start, unit), size)


def flip(matrix):
    return matrix.astype(f32).T.astype(matrix.dtype)


class Wire:
    def __init__(self, send_sems, recv_sems):
        self.send_sems, self.recv_sems, self.used, self.sent = send_sems, recv_sems, 0, []

    def copy(self, index, src, dst, device):
        return pltpu.make_async_remote_copy(
            src_ref=src, dst_ref=dst, send_sem=self.send_sems.at[index], recv_sem=self.recv_sems.at[index],
            device_id=device, device_id_type=MESH,
        )

    def send(self, src, dst, device):
        index = self.used
        self.used += 1
        copy = self.copy(index, src, dst, device)
        copy.start()
        self.sent.append(copy)
        return index

    def receive(self, index, ref, device):
        self.copy(index, ref, ref, device).wait_recv()

    def drain(self):
        for copy in self.sent:
            copy.wait_send()
        self.sent = []


def layer(
    lengths, order, tokens, cot, w_out, w_up, w_down, w_query, w_key, w_value,
    g_attn, g_mlp, q_scale, b_up, b_down,
    layer_out, input_grad, grad_mlp, grad_qkv, small_out,
    later_weights,
    weights, shards, gathered, wqkv_all, wqkv_t, raw_q, qkv_slot, qkv_pos, raw_pos, k_rows, v_rows, probs, out_pos,
    head_send, mixed_t, dout_t, dout_slot, dout_pos, dk_acc, dv_acc, grads_pos, grads_flat, grads_in,
    acts, up_in, up_all, t1, r1, t2, r2, t3, r3, swap_out, rows_out, rows_in,
    gw, gw_send, gw_in, gq_send, gq_in, ar_own, ar_half, ar_slots, ar_total,
    local_sems, send_sems, recv_sems,
):
    c, f = lax.axis_index("ctx"), lax.axis_index("fsdp")
    y_hi, x, core = c // 8, (c // 2) % 4, c % 2
    z, y_lo = f // 2, f % 2
    y = 2 * y_hi + y_lo

    def at(x_at, y_at, z_at, core_at):
        return ((y_at // 2) * 8 + x_at * 2 + core_at, z_at * 2 + y_at % 2)

    def away(dx=0, dy=0, dz=0):
        return at((x + dx) % 4, (y + dy) % 4, (z + dz) % 4, core)

    sibling = (c + 1 - 2 * core, f)
    wire = Wire(send_sems, recv_sems)

    axes = {0: "xzy", 1: "yxz", 2: "zyx"}
    here = {"x": x, "y": y, "z": z}

    def final_target(w):
        a, b, last = (here[n] for n in axes[w])
        return (4 * a + b, 2 * last + core)

    def final_source(w):
        found = dict(zip(axes[w], (c // 4, c % 4, f // 2)))
        return at(found["x"], found["y"], found["z"], f % 2)

    own_rows = ds(f * SHARD, SHARD, SHARD)
    loads = []
    for j, ref in enumerate((w_query, w_key, w_value, w_out, w_up, w_down)):
        load = pltpu.make_async_copy(
            ref, shards.at[j] if j < 3 else weights.at[j - 3, own_rows], local_sems.at[j]
        )
        load.start()
        loads.append(load)

    barrier = pltpu.get_barrier_semaphore()
    peers = [((c + k) % 16, f) for k in range(1, 16)] + [(c, (f + k) % 8) for k in range(1, 8)]
    peers.append(at(x, 3 - y, z, core))
    for w in range(3):
        peers += [final_target(w), final_source(w)]
    for peer in peers:
        pl.semaphore_signal(barrier, inc=1, device_id=peer, device_id_type=MESH)

    gain_one, gain_two = g_attn[...].reshape(1, D), g_mlp[...].reshape(1, D)
    bias_up, bias_down = b_up[...].reshape(1, D), b_down[...].reshape(1, D)
    x_in = tokens[...].astype(f32)
    r_one = lax.rsqrt(jnp.mean(x_in * x_in, axis=1, keepdims=True) + EPS)
    gathered[ds(c * BLK, BLK, BLK), :] = (x_in * r_one * gain_one).astype(bf16)
    scale = QUERY_CONST * jnp.log(1.0 + jnp.exp(q_scale[...].reshape(1, HEAD_DIM)))
    scale_col = jnp.broadcast_to(scale, (BLK, HEAD_DIM)).T[:, :1]

    from_col = lax.broadcasted_iota(jnp.int32, (D, 256), 0) - c * HEAD_DIM
    to_col = lax.broadcasted_iota(jnp.int32, (D, 256), 1)
    own_cols = jnp.zeros((SHARD, 256), f32)
    for j in range(3):
        loads[j].wait()
        pick = (from_col >= 0) & (from_col < HEAD_DIM) & (to_col == from_col + j * HEAD_DIM)
        own_cols = own_cols + nn(shards[j], jnp.where(pick, 1.0, 0.0).astype(bf16))
    wqkv_all[own_rows, :] = own_cols.astype(bf16)
    keep = pltpu.make_async_copy(shards, later_weights.at[:, own_rows], local_sems.at[6])
    keep.start()

    pl.semaphore_wait(barrier, len(peers))

    def piece(yh, xa, co, part=None):
        start = ((yh * 4 + xa) * 2 + co) * BLK
        if part is None:
            return gathered.at[ds(start, BLK, BLK)]
        return gathered.at[ds(start + part * 64, 64, 64)]

    other = 1 - y_hi
    xl, xr, xo = (x + 3) % 4, (x + 1) % 4, (x + 2) % 4
    def pass_chunk(yh, xa, part, device):
        chunk = piece(yh, xa, core, part)
        return wire.send(chunk, chunk, device)

    left, right, across = away(dx=3), away(dx=1), away(dy=2)
    to_y, to_xr, to_xl = {}, {}, {}
    for one, other_one in ((0, 1), (1, 0)):
        to_y[one] = pass_chunk(y_hi, x, one, across)
        to_xr[one] = pass_chunk(y_hi, x, one, right)
        to_xl[other_one] = pass_chunk(y_hi, x, other_one, left)
    to_core = wire.send(piece(y_hi, x, core), piece(y_hi, x, core), sibling)

    def columns_at(zz, lo):
        return wqkv_all.at[ds((zz * 2 + lo) * SHARD, SHARD, SHARD)]

    def columns_round_z(lo):
        return [wire.send(columns_at(z, lo), columns_at(z, lo), away(dz=k)) for k in (1, 3, 2)]

    pair = (c, f + 1 - 2 * y_lo)
    cols_y = wire.send(columns_at(z, y_lo), columns_at(z, y_lo), pair)
    cols_z = columns_round_z(y_lo)

    half_cols = ds(core * HALF, HALF, 128)
    across_y = (y + 1 + 2 * core) % 4
    from_y = (y + 3 + 2 * core) % 4

    def rows_of(view, zz, lo, first=0, count=SHARD):
        buffer, at_first, number = view
        return buffer.at[pl.ds(at_first, number), ds((zz * 2 + lo) * SHARD + first, count, 16), half_cols]

    zl, zr, zo = (z + 3) % 4, (z + 1) % 4, (z + 2) % 4

    class Gather:
        def __init__(self, buffer, own, split):
            self.buffer, self.own, self.split = buffer, own, split
            self.first, self.count, self.left = (80 * (x % 2), 80, 48) if split else (0, SHARD, 80)
            self.kept, self.over_x = [], []

        def rows(self, zz, lo, part=None):
            first, count = self.first, self.count
            if part is not None:
                first, count = (first, self.left) if part == 0 else (first + self.left, count - self.left)
            return rows_of(self.buffer, zz, lo, first, count)

        def begin(self):
            own, one = self.own(self.first, self.count), self.rows(z, y_lo)
            self.r0 = wire.send(own, one, away(dz=1))
            self.l0 = wire.send(own, one, away(dz=3))

        def begin_y(self):
            self.y = wire.send(self.own(self.first, self.count), self.rows(z, y_lo), at(x, across_y, z, core))

        def give(self, zz, lo):
            ref = self.rows(zz, lo)
            self.kept.append((wire.send(ref, ref, sibling), ref))
            if self.split:
                self.over_x.append((wire.send(ref, ref, at((x + 1 + 2 * core) % 4, y, z, core)), zz, lo))

        def second(self):
            two = self.rows(z, 1 - y_lo)
            wire.receive(self.y, two, at(x, from_y, z, core))
            self.r1 = wire.send(two, two, away(dz=1))
            self.l1 = wire.send(two, two, away(dz=3))
            self.give(z, 1 - y_lo)

        def forward(self, lo, left, right):
            wire.receive(right, self.rows(zl, lo), away(dz=3))
            one = self.rows(zl, lo, 0)
            to_right = wire.send(one, one, away(dz=1))
            wire.receive(left, self.rows(zr, lo), away(dz=1))
            two = self.rows(zr, lo, 1)
            to_left = wire.send(two, two, away(dz=3))
            self.give(zl, lo)
            self.give(zr, lo)
            return to_right, to_left

        def third(self):
            self.f0 = self.forward(y_lo, self.l0, self.r0)

        def fourth(self):
            self.f1 = self.forward(1 - y_lo, self.l1, self.r1)

        def last(self, lo, pair):
            wire.receive(pair[0], self.rows(zo, lo, 0), away(dz=3))
            wire.receive(pair[1], self.rows(zo, lo, 1), away(dz=1))
            self.give(zo, lo)

        def fifth(self):
            self.last(y_lo, self.f0)

        def sixth(self):
            self.last(1 - y_lo, self.f1)

        def seventh(self):
            for index, zz, lo in self.over_x:
                ref = rows_of(self.buffer, zz, lo, 80 - self.first, 80)
                wire.receive(index, ref, at((x + 3 + 2 * core) % 4, y, z, core))
                self.kept.append((wire.send(ref, ref, sibling), ref))

        def finish(self):
            for index, ref in self.kept:
                wire.receive(index, ref, sibling)

    def early(j, split):
        view = (weights, j, 1)
        return Gather(view, lambda first, count: rows_of(view, z, y_lo, first, count), split)

    out_rows, up_rows, down_rows = early(0, False), early(1, True), early(2, True)
    second_set = Gather((later_weights, 0, 3), lambda first, count: shards.at[:, ds(first, count, 16), half_cols], True)
    for load in loads[3:]:
        load.wait()
    out_rows.begin()

    def project(yh, xa):
        chip = yh * 4 + xa
        both = nt(wqkv_t[...], gathered[ds(chip * TILE, TILE, TILE), :])
        for i in range(2):
            one = both[:, i * BLK:(i + 1) * BLK]
            raw_q[2 * chip + i] = one[:HEAD_DIM]
            qkv_slot[2 * chip + i, :HEAD_DIM] = (one[:HEAD_DIM] * scale_col).astype(bf16)
            qkv_slot[2 * chip + i, HEAD_DIM:] = one[HEAD_DIM:240].astype(bf16)

    def take(indices, yh, xa, device, parts=(0, 1)):
        for part in parts:
            wire.receive(indices[part], piece(yh, xa, core, part), device)

    def to_sibling(yh, xa):
        return wire.send(piece(yh, xa, core), piece(yh, xa, core), sibling)

    def both_cores(index, yh, xa):
        wire.receive(index, piece(yh, xa, 1 - core), sibling)
        project(yh, xa)

    wire.receive(cols_y, columns_at(z, 1 - y_lo), pair)
    cols_yz = columns_round_z(1 - y_lo)
    down_rows.begin()
    up_rows.begin()
    ring, y_r, y_l = {}, {}, {}
    take(to_xr, y_hi, xl, left, (0,))
    ring[0] = pass_chunk(y_hi, xl, 0, right)
    take(to_xl, y_hi, xr, right, (1,))
    ring[1] = pass_chunk(y_hi, xr, 1, left)
    take(to_y, other, x, across, (0,))
    y_r[0] = pass_chunk(other, x, 0, right)
    y_l[0] = pass_chunk(other, x, 0, left)
    take(to_xr, y_hi, xl, left, (1,))
    core_l = to_sibling(y_hi, xl)
    take(to_xl, y_hi, xr, right, (0,))
    core_r = to_sibling(y_hi, xr)
    take(to_y, other, x, across, (1,))
    y_r[1] = pass_chunk(other, x, 1, right)
    y_l[1] = pass_chunk(other, x, 1, left)
    core_y = to_sibling(other, x)
    out_rows.begin_y()
    down_rows.begin_y()
    up_rows.begin_y()
    for index, k in zip(cols_z, (1, 3, 2)):
        wire.receive(index, columns_at((z + 4 - k) % 4, y_lo), away(dz=4 - k))
    for index, k in zip(cols_yz, (1, 3, 2)):
        wire.receive(index, columns_at((z + 4 - k) % 4, 1 - y_lo), away(dz=4 - k))
    wqkv_t[...] = flip(wqkv_all[...])
    far = {}
    wire.receive(ring[0], piece(y_hi, xo, core, 0), left)
    far[0] = pass_chunk(y_hi, xo, 0, across)
    wire.receive(ring[1], piece(y_hi, xo, core, 1), right)
    far[1] = pass_chunk(y_hi, xo, 1, across)
    core_o = to_sibling(y_hi, xo)
    both_cores(to_core, y_hi, x)
    both_cores(core_l, y_hi, xl)
    out_rows.second()
    out_rows.third()
    both_cores(core_r, y_hi, xr)
    both_cores(core_y, other, x)
    both_cores(core_o, y_hi, xo)
    take(y_r, other, xl, left)
    core_yl = to_sibling(other, xl)
    take(y_l, other, xr, right)
    core_yr = to_sibling(other, xr)
    down_rows.second()
    up_rows.second()
    both_cores(core_yl, other, xl)
    both_cores(core_yr, other, xr)
    take(far, other, xo, across)
    core_f = to_sibling(other, xo)
    out_rows.fourth()
    both_cores(core_f, other, xo)

    waiting = [
        down_rows.third, up_rows.third, second_set.begin_y, second_set.begin, out_rows.fifth, down_rows.fourth,
        up_rows.fourth, out_rows.sixth, down_rows.fifth, up_rows.fifth, down_rows.sixth, up_rows.sixth,
    ]

    def move_on(number):
        for _ in range(number):
            if waiting:
                waiting.pop(0)()

    slot_of = []
    for p in range(NBLK):
        slot = 0
        for b in range(NBLK):
            slot = jnp.where(order[0, b] == p, b, slot)
        slot_of.append(slot)
    for p in range(NBLK):
        qkv_pos[:, p * BLK:(p + 1) * BLK] = qkv_slot[slot_of[p]]
        raw_pos[:, p * BLK:(p + 1) * BLK] = raw_q[slot_of[p]]
    k_rows[...] = flip(qkv_pos[HEAD_DIM:2 * HEAD_DIM, :])
    v_rows[...] = flip(qkv_pos[2 * HEAD_DIM:, :])

    ends, total = [], 0
    for s in range(4):
        total = total + lengths[0, s]
        ends.append(total)

    at_part = 0
    parts_of = []
    for t in range(GROUP // TILE):
        low, high = max(0, t * TILE - WINDOW), (t + 1) * TILE
        width = high - low
        tile = slice(t * TILE, high)
        scores = nn(k_rows[low:high, :], qkv_pos[:HEAD_DIM, tile])
        at_q = t * TILE + lax.broadcasted_iota(jnp.int32, (1, TILE), 1)
        start = jnp.zeros((1, TILE), jnp.int32)
        for end in ends:
            start = jnp.where(at_q >= end, end, start)
        at_k = low + lax.broadcasted_iota(jnp.int32, (width, TILE), 0)
        scores = jnp.where((at_k <= at_q) & (at_k >= start), scores, MASKED)
        top = jnp.max(scores, axis=0, keepdims=True)
        powers = jnp.exp(scores - top)
        part = powers * (1.0 / jnp.sum(powers, axis=0, keepdims=True))
        part = part.astype(bf16)
        parts_of.append(slice(at_part, at_part + width))
        at_part += width
        probs[parts_of[t], :] = part
        out = nn(qkv_pos[2 * HEAD_DIM:, low:high], part).astype(bf16)
        out_pos[2 * t] = out[:, :BLK]
        out_pos[2 * t + 1] = out[:, BLK:]
        move_on(1)

    for b in range(NBLK):
        head_send[b] = out_pos[order[0, b]]

    def exchange(src_of, dst):
        return [wire.send(src_of((c + k) % 16), dst, ((c + k) % 16, f)) for k in range(1, 16)]

    def arrive(indices, dst_of):
        for k, index in enumerate(indices):
            src = (c + 15 - k) % 16
            wire.receive(index, dst_of(src), (src, f))

    head_rows = ds(c * HEAD_DIM, HEAD_DIM, HEAD_DIM)
    mixing = exchange(lambda b: head_send.at[b], mixed_t.at[head_rows])
    mixed_t[head_rows, :] = head_send[c]
    move_on(len(waiting))
    down_rows.seventh()
    up_rows.seventh()
    second_set.second()
    down_rows.finish()

    cot_f = cot[...].astype(f32)

    def spread(a, w):
        return jnp.concatenate([nn(a, weights[w, :, n:n + 256]) for n in range(0, D, 256)], axis=1)

    def spread_back(a, w):
        return jnp.concatenate([nt(a, weights[w, n:n + 256, :]) for n in range(0, D, 256)], axis=1)

    grad_active = spread_back(cot[...], 2)
    arrive(mixing, lambda src: mixed_t.at[ds(src * HEAD_DIM, HEAD_DIM, HEAD_DIM)])

    out_rows.finish()
    mixed = flip(mixed_t[...])
    after = x_in + spread(mixed, 0)
    r_two = lax.rsqrt(jnp.mean(after * after, axis=1, keepdims=True) + EPS)
    n_two = after * r_two
    normed_two = (n_two * gain_two).astype(bf16)
    up_rows.finish()
    wire.set_one = len(wire.sent)
    hidden = spread(normed_two, 1) + bias_up
    gate = jax.nn.sigmoid(hidden)
    active = (hidden * gate).astype(bf16)
    grad_hidden = (grad_active * gate * (1.0 + hidden * (1.0 - gate))).astype(bf16)
    back_two = spread_back(grad_hidden, 1)
    scaled = back_two * gain_two
    grad_after = cot_f + r_two * (scaled - n_two * jnp.mean(scaled * n_two, axis=1, keepdims=True))
    grad_branch = grad_after.astype(bf16)
    dout_t[...] = flip(spread_back(grad_branch, 0).astype(bf16))
    douts = exchange(lambda b: dout_t.at[ds(b * HEAD_DIM, HEAD_DIM, HEAD_DIM)], dout_slot.at[c])
    dout_slot[c] = dout_t[head_rows, :]

    my_lanes = ds(core * BLK, BLK, BLK)
    other_half = ds((1 - core) * HALF, HALF, 128)
    ups = (grad_branch, grad_hidden, cot[...])
    acts[0, :, my_lanes] = mixed_t[...]
    acts[1, :, my_lanes] = flip(normed_two)
    acts[2, :, my_lanes] = flip(active)
    for w in range(3):
        up_in[w] = ups[w]
    give_acts = wire.send(acts.at[:, :, my_lanes], acts.at[:, :, my_lanes], sibling)
    give_up = wire.send(up_in.at[:, :, other_half], up_all.at[:, my_lanes], sibling)
    for w in range(3):
        up_all[w, my_lanes, :] = up_in[w, :, half_cols]
    layer_out[...] = (after + spread(active, 2) + bias_down).astype(bf16)
    input_grad[...] = grad_after
    ar_own[...] = jnp.zeros_like(ar_own)
    ar_own[1:2, :] = jnp.sum(back_two * n_two, axis=0, keepdims=True)
    ar_own[2:3, :] = jnp.sum(grad_hidden.astype(f32), axis=0, keepdims=True)
    ar_own[3:4, :] = jnp.sum(cot_f, axis=0, keepdims=True)

    second_set.third()
    sib_lanes = ds((1 - core) * BLK, BLK, BLK)
    wire.receive(give_acts, acts.at[:, :, sib_lanes], sibling)
    wire.receive(give_up, up_all.at[:, sib_lanes], sibling)

    def scatter(w, stage, src_of, dst_of):
        axis = axes[w][stage]
        return [
            wire.send(src_of((here[axis] + k) % 4), dst_of(k - 1), away(**{"d" + axis: k})) for k in range(1, 4)
        ]

    def gathered_sum(w, stage, indices, first, buffers):
        axis = axes[w][stage]
        for k, index in enumerate(indices):
            wire.receive(index, buffers.at[w, k], away(**{"d" + axis: 3 - k}))
        return first.astype(f32) + buffers[w, 0].astype(f32) + buffers[w, 1].astype(f32) + buffers[w, 2].astype(f32)

    stage_one, stage_two, stage_three = {}, {}, {}
    for w in (2, 1, 0):
        for n in range(0, D, 320):
            rows = slice(n, n + 320)
            t1[w, rows, :] = nn(acts[w, rows, :], up_all[w]).astype(bf16)
        stage_one[w] = scatter(w, 0, lambda d: t1.at[w, ds(d * 320, 320, 320)], lambda k: r1.at[w, k])

    def second_stage(w):
        mine = t1[w, ds(here[axes[w][0]] * 320, 320, 320), :]
        t2[w] = gathered_sum(w, 0, stage_one[w], mine, r1).astype(bf16)
        stage_two[w] = scatter(w, 1, lambda d: t2.at[w, ds(d * 80, 80, 80)], lambda k: r2.at[w, k])

    def third_stage(w):
        mine = t2[w, ds(here[axes[w][1]] * 80, 80, 80), :]
        both = gathered_sum(w, 1, stage_two[w], mine, r2)
        for d in range(4):
            t3[w, d] = jnp.concatenate([both[20 * d:20 * d + 20], jnp.zeros((12, HALF), f32)], axis=0).astype(bf16)
        stage_three[w] = scatter(w, 2, lambda d: t3.at[w, d], lambda k: r3.at[w, k])

    def fourth_stage(w):
        both = gathered_sum(w, 2, stage_three[w], t3[w, here[axes[w][2]]], r3)
        for i in range(2):
            swap_out[w, i] = jnp.concatenate([both[10 * i:10 * i + 10], jnp.zeros((6, HALF), f32)], axis=0)
        rows_out[w, :, half_cols] = swap_out[w, core]
        return wire.send(swap_out.at[w, 1 - core], rows_out.at[w, :, half_cols], sibling)

    second_set.fourth()
    arrive(douts, lambda src: dout_slot.at[src])

    for p in range(NBLK):
        dout_pos[:, p * BLK:(p + 1) * BLK] = dout_slot[slot_of[p]]
    dk_acc[...] = jnp.zeros_like(dk_acc)
    dv_acc[...] = jnp.zeros_like(dv_acc)
    scale_terms = jnp.zeros((HEAD_DIM, 1), f32)
    for t in range(GROUP // TILE):
        low, high = max(0, t * TILE - WINDOW), (t + 1) * TILE
        width = high - low
        tile = slice(t * TILE, high)
        d_out = dout_pos[:, tile]
        delta = jnp.sum(d_out.astype(f32) * jnp.concatenate([out_pos[2 * t], out_pos[2 * t + 1]], axis=1).astype(f32), axis=0, keepdims=True)
        part = probs[parts_of[t], :]
        d_probs = nn(v_rows[low:high, :], d_out)
        d_scores = (part.astype(f32) * (d_probs - delta)).astype(bf16)
        dq = nn(qkv_pos[HEAD_DIM:2 * HEAD_DIM, low:high], d_scores)
        scale_terms = scale_terms + jnp.sum(dq * raw_pos[:, tile], axis=1, keepdims=True)
        dq = (dq * scale_col).astype(bf16)
        grads_pos[2 * t, :HEAD_DIM] = dq[:, :BLK]
        grads_pos[2 * t + 1, :HEAD_DIM] = dq[:, BLK:]
        if t in (3, 6):
            (second_set.fifth, second_set.sixth)[t // 4]()
        dk_acc[:, low:high] += nt(qkv_pos[:HEAD_DIM, tile], d_scores)
        dv_acc[:, low:high] += nt(d_out, part)

    for p in range(NBLK):
        lanes = slice(p * BLK, (p + 1) * BLK)
        grads_pos[p, HEAD_DIM:2 * HEAD_DIM] = dk_acc[:, lanes].astype(bf16)
        grads_pos[p, 2 * HEAD_DIM:] = dv_acc[:, lanes].astype(bf16)
    for b in range(NBLK):
        block = grads_pos[order[0, b]]
        qkv_slot[b] = block
        grads_flat[:, b * BLK:(b + 1) * BLK] = block
    sent_grads = exchange(lambda b: qkv_slot.at[b], grads_in.at[c])
    grads_in[c] = qkv_slot[c]

    for n in range(0, D, 256):
        grad_t = nn(grads_flat[...], gathered[:, n:n + 256])
        by_gain = jnp.sum(wqkv_t[:240, n:n + 256].astype(f32) * grad_t, axis=0, keepdims=True)
        ar_own[0:1, n:n + 256] = by_gain / gain_one[:, n:n + 256]
        gw[n:n + 256, :] = jnp.concatenate([grad_t, jnp.zeros((16, 256), f32)], axis=0).T
    for fs in range(8):
        picked = [gw[cs * 80 + fs * 10:cs * 80 + fs * 10 + 10, :] for cs in range(16)]
        gw_send[fs] = jnp.concatenate(picked, axis=0).astype(bf16)
    ar_own[4:5, :HEAD_DIM] = jnp.broadcast_to(scale_terms, (HEAD_DIM, BLK)).T[:1]
    half_sums = wire.send(ar_own.at[:, other_half], ar_half, sibling)
    shares = [wire.send(gw_send.at[(f + k) % 8], gw_in.at[k - 1], (c, (f + k) % 8)) for k in range(1, 8)]

    def spread_sums(i, axis, value):
        me = here[axis]
        ar_slots[i, me] = value
        return [wire.send(ar_slots.at[i, me], ar_slots.at[i, me], away(**{"d" + axis: k})) for k in range(1, 4)]

    def collect_sums(i, axis, indices):
        for k, index in enumerate(indices):
            wire.receive(index, ar_slots.at[i, (here[axis] + 3 - k) % 4], away(**{"d" + axis: 3 - k}))
        return ar_slots[i, 0] + ar_slots[i, 1] + ar_slots[i, 2] + ar_slots[i, 3]

    wire.receive(half_sums, ar_half, sibling)
    sums = spread_sums(0, "x", ar_own[:, half_cols] + ar_half[...])
    second_set.seventh()
    second_stage(2)
    sums = spread_sums(1, "y", collect_sums(0, "x", sums))
    second_stage(1)
    second_stage(0)
    sums = spread_sums(2, "z", collect_sums(1, "y", sums))

    for k, index in enumerate(shares):
        src_f = (f + 7 - k) % 8
        wire.receive(index, gw_in.at[k], (c, src_f))
    both = gw_send[f].astype(f32)
    for k in range(7):
        both = both + gw_in[k].astype(f32)
    for cs in range(16):
        gq_send[cs] = jnp.concatenate([both[10 * cs:10 * cs + 10], jnp.zeros((6, 256), f32)], axis=0).astype(bf16)
    gq_in[c] = gq_send[c]
    heads = exchange(lambda b: gq_send.at[b], gq_in.at[c])
    third_stage(2)
    third_stage(1)
    third_stage(0)
    ar_total[:, half_cols] = collect_sums(2, "z", sums)
    half_sums = wire.send(ar_total.at[:, half_cols], ar_total.at[:, half_cols], sibling)

    second_set.finish()
    for copy in wire.sent[:wire.set_one]:
        copy.wait_send()
    wire.sent = wire.sent[wire.set_one:]
    keep.wait()
    loads = []
    for j in range(3):
        load = pltpu.make_async_copy(later_weights.at[j], weights.at[j], local_sems.at[j])
        load.start()
        loads.append(load)
    arrive(sent_grads, lambda src: grads_in.at[src])
    grad_normed = jnp.zeros((BLK, D), f32)
    for j in range(3):
        loads[j].wait()
        rows = slice(j * HEAD_DIM, (j + 1) * HEAD_DIM)
        joined = jnp.concatenate([grads_in[h, rows] for h in range(HEADS)], axis=0)
        grad_normed = grad_normed + spread_back(flip(joined), j)
    n_one = x_in * r_one
    scaled = grad_normed * gain_one
    through = r_one * (scaled - n_one * jnp.mean(scaled * n_one, axis=1, keepdims=True))
    input_grad[...] = input_grad[...] + through

    swaps = [(w, fourth_stage(w)) for w in (2, 1, 0)]
    finals = []
    for w, index in swaps:
        wire.receive(index, rows_out.at[w, :, other_half], sibling)
        target = final_target(w)
        index = wire.used
        wire.used += 1
        stays = (target[0] == c) & (target[1] == f)
        copy = wire.copy(index, rows_out.at[w], rows_in.at[w], target)
        within = pltpu.make_async_copy(rows_out.at[w], rows_in.at[w], recv_sems.at[index])
        pl.when(jnp.logical_not(stays))(copy.start)
        pl.when(stays)(within.start)
        finals.append((w, index, copy, stays))

    wire.receive(half_sums, ar_total.at[:, other_half], sibling)
    small_out[...] = ar_total[...]
    arrive(heads, lambda src: gq_in.at[src])
    grad_qkv[...] = gq_in[...]
    for w, index, copy, stays in finals:
        wire.receive(index, rows_in.at[w], final_source(w))
        pl.when(jnp.logical_not(stays))(copy.wait_send)
    grad_mlp[...] = rows_in[...]
    wire.drain()
    assert wire.used <= N_SEM


def outputs(
    out, in_grad, rows, qkv, small, q_scale,
    layer_out, input_grad, g_query, g_key, g_value, g_out, g_up, g_down, g_gain_one, g_gain_two, g_scale, g_bias_up, g_bias_down,
    rows_here, qkv_here, small_here, sems,
):
    places = (layer_out.at[0], input_grad.at[0], rows_here, qkv_here, small_here)
    copies = [
        pltpu.make_async_copy(src, dst, sems.at[i]) for i, (src, dst) in enumerate(zip((out, in_grad, rows, qkv, small), places))
    ]
    for copy in copies:
        copy.start()
    for copy in copies:
        copy.wait()
    rows, qkv, small = rows_here, qkv_here, small_here
    for j, ref in enumerate((g_query, g_key, g_value)):
        tiles = [jnp.zeros((16, BLK), f32) for _ in range(11)]
        for h in range(HEADS):
            tile, start = divmod(h * HEAD_DIM, BLK)
            moved = pltpu.roll(qkv[h].astype(f32), (start - j * HEAD_DIM) % 256, 1)
            lane = lax.broadcasted_iota(jnp.int32, (16, 256), 1)
            moved = jnp.where((lane >= start) & (lane < start + HEAD_DIM), moved, 0.0)
            tiles[tile] = tiles[tile] + moved[:, :BLK]
            tiles[tile + 1] = tiles[tile + 1] + moved[:, BLK:]
        ref[...] = jnp.concatenate(tiles[:10], axis=1)[:10]
    for w, ref in enumerate((g_out, g_up, g_down)):
        ref[...] = rows[w, :10, :]
    for i, ref in ((0, g_gain_one), (1, g_gain_two), (2, g_bias_up), (3, g_bias_down)):
        ref[...] = small[i, :]
    g_scale[...] = small[4, :HEAD_DIM] * QUERY_CONST * jax.nn.sigmoid(q_scale[...])


def on_device(
    tokens, cotangent, lengths, block_order, w_query, w_key, w_value, w_out, w_up, w_down,
    g_attn, g_mlp, q_scale, b_up, b_down,
):
    vmem, smem, any_space = (pl.BlockSpec(memory_space=s) for s in (pltpu.VMEM, pltpu.SMEM, pl.ANY))
    shapes = {
        "weights": ((3, D, D), bf16), "shards": ((3, SHARD, D), bf16), "gathered": ((GROUP, D), bf16), "wqkv_all": ((D, 256), bf16),
        "wqkv_t": ((256, D), bf16), "raw_q": ((NBLK, HEAD_DIM, BLK), f32), "qkv_slot": ((NBLK, 240, BLK), bf16),
        "qkv_pos": ((240, GROUP), bf16), "raw_pos": ((HEAD_DIM, GROUP), f32), "k_rows": ((GROUP, HEAD_DIM), bf16),
        "v_rows": ((GROUP, HEAD_DIM), bf16), "probs": ((7680, TILE), bf16), "out_pos": ((NBLK, HEAD_DIM, BLK), bf16),
        "head_send": ((NBLK, HEAD_DIM, BLK), bf16), "mixed_t": ((D, BLK), bf16), "dout_t": ((D, BLK), bf16),
        "dout_slot": ((NBLK, HEAD_DIM, BLK), bf16), "dout_pos": ((HEAD_DIM, GROUP), bf16),
        "dk_acc": ((HEAD_DIM, GROUP), f32), "dv_acc": ((HEAD_DIM, GROUP), f32), "grads_pos": ((NBLK, 240, BLK), bf16),
        "grads_flat": ((240, GROUP), bf16), "grads_in": ((NBLK, 240, BLK), bf16),
        "acts": ((3, D, 2 * BLK), bf16), "up_in": ((3, BLK, D), bf16), "up_all": ((3, 2 * BLK, HALF), bf16),
        "t1": ((3, D, HALF), bf16), "r1": ((3, 3, 320, HALF), bf16), "t2": ((3, 320, HALF), bf16),
        "r2": ((3, 3, 80, HALF), bf16), "t3": ((3, 4, 32, HALF), bf16), "r3": ((3, 3, 32, HALF), bf16),
        "swap_out": ((3, 2, 16, HALF), f32), "rows_out": ((3, 16, D), f32), "rows_in": ((3, 16, D), f32),
        "gw": ((D, 256), f32), "gw_send": ((8, SHARD, 256), bf16), "gw_in": ((7, SHARD, 256), bf16),
        "gq_send": ((16, 16, 256), bf16), "gq_in": ((16, 16, 256), bf16),
        "ar_own": ((8, D), f32), "ar_half": ((8, HALF), f32), "ar_slots": ((3, 4, 8, HALF), f32),
        "ar_total": ((8, D), f32),
    }
    outs = {
        "layer_out": ((BLK, D), bf16), "input_grad": ((BLK, D), f32), "grad_mlp": ((3, 16, D), f32),
        "grad_qkv": ((16, 16, 256), bf16), "small_out": ((8, D), f32), "later_weights": ((3, D, D), bf16),
    }
    ins = (
        "lengths", "order", "tokens", "cot", "w_out", "w_up", "w_down", "w_query", "w_key", "w_value",
        "g_attn", "g_mlp", "q_scale", "b_up", "b_down",
    )

    def body(*refs):
        names = ins + tuple(outs) + tuple(shapes) + ("local_sems", "send_sems", "recv_sems")
        layer(**dict(zip(names, refs, strict=True)))

    out, in_grad, rows, qkv, small, _ = pl.pallas_call(
        body,
        out_shape=[jax.ShapeDtypeStruct(*s) for s in outs.values()],
        in_specs=[smem, smem] + [vmem] * 2 + [any_space] * 6 + [vmem] * 5,
        out_specs=[vmem] * (len(outs) - 1) + [any_space],
        scratch_shapes=[pltpu.VMEM(*s) for s in shapes.values()]
        + [pltpu.SemaphoreType.DMA((7,)), pltpu.SemaphoreType.DMA((N_SEM,)), pltpu.SemaphoreType.DMA((N_SEM,))],
        compiler_params=pltpu.CompilerParams(
            collective_id=0, has_side_effects=True, vmem_limit_bytes=62 << 20
        ),
    )(
        lengths, block_order, tokens[0], cotangent[0], w_out, w_up, w_down, w_query, w_key, w_value,
        g_attn, g_mlp, q_scale, b_up, b_down,
    )
    row = jax.ShapeDtypeStruct((10, D), f32)
    vector = jax.ShapeDtypeStruct((D,), f32)
    return pl.pallas_call(
        outputs,
        out_shape=[
            jax.ShapeDtypeStruct((1, BLK, D), bf16), jax.ShapeDtypeStruct((1, BLK, D), f32), *[row] * 6,
            vector, vector, jax.ShapeDtypeStruct((HEAD_DIM,), f32), vector, vector,
        ],
        in_specs=[any_space] * 5 + [vmem],
        out_specs=[vmem] * 13,
        scratch_shapes=[
            pltpu.VMEM((3, 16, D), f32), pltpu.VMEM((16, 16, 256), bf16), pltpu.VMEM((8, D), f32),
            pltpu.SemaphoreType.DMA((5,)),
        ],
        compiler_params=pltpu.CompilerParams(vmem_limit_bytes=62 << 20),
    )(out, in_grad, rows, qkv, small, q_scale)


def solution(mesh):
    tokens, rows, whole = P("fsdp", "ctx", None), P("fsdp", None), P()
    owned = P(("ctx", "fsdp"), None)
    return jax.shard_map(
        on_device, mesh=mesh,
        in_specs=(tokens, tokens, rows, rows) + (rows,) * 6 + (whole,) * 5,
        out_specs=(tokens, tokens) + (owned,) * 6 + (whole,) * 5,
        check_vma=False,
    )
```

```python
import functools
import math

import jax
import jax.numpy as jnp
from jax import lax
from jax.experimental import pallas as pl
from jax.experimental.pallas import tpu as pltpu
from jax.sharding import PartitionSpec as P

D = 1280
HEADS = 16
HEAD_DIM = 80
BLK = 128
GROUP = 2048
NBLK = 16
SHARD = 160
HALF = 640
TILE = 256
WINDOW = 1024
EPS = 1e-06
QUERY_CONST = 1.442695 / math.sqrt(HEAD_DIM)
MASKED = -1e30
N_SEM = 288
ORDERS = (("yxz", "yxz"), ("xzy", "xzy"), ("zyx", "zyx"))
MESH = pl.DeviceIdType.MESH
bf16, f32 = jnp.bfloat16, jnp.float32


def nn(a, b):
    return jnp.dot(a, b, preferred_element_type=f32)


def nt(a, b):
    return lax.dot_general(a, b, (((1,), (1,)), ((), ())), preferred_element_type=f32)


def ds(start, size, unit):
    return pl.ds(pl.multiple_of(start, unit), size)


def flip(matrix):
    return matrix.astype(f32).T.astype(matrix.dtype)


class Wire:
    def __init__(self, send_sems, recv_sems):
        self.send_sems, self.recv_sems, self.used, self.sent = send_sems, recv_sems, 0, []

    def copy(self, index, src, dst, device):
        return pltpu.make_async_remote_copy(
            src_ref=src, dst_ref=dst, send_sem=self.send_sems.at[index], recv_sem=self.recv_sems.at[index],
            device_id=device, device_id_type=MESH,
        )

    def send(self, src, dst, device):
        index = self.used
        self.used += 1
        copy = self.copy(index, src, dst, device)
        copy.start()
        self.sent.append(copy)
        return index

    def receive(self, index, ref, device):
        self.copy(index, ref, ref, device).wait_recv()

    def drain(self):
        for copy in self.sent:
            copy.wait_send()
        self.sent = []


def layer(
    lengths, order, tokens, cot, w_out, w_up, w_down, w_query, w_key, w_value,
    g_attn, g_mlp, q_scale, b_up, b_down,
    layer_out, input_grad, grad_mlp, grad_qkv, small_out,
    later_weights,
    weights, shards, gathered, wqkv_all, wqkv_t, raw_q, qkv_slot, qkv_pos, raw_pos, k_rows, v_rows, probs, out_pos,
    head_send, mixed_t, dout_t, dout_slot, dout_pos, dk_acc, dv_acc, grads_pos, grads_flat, grads_in,
    acts, up_in, up_all, t1, r1, t2, r2, t3, r3, rows_out, rows_in,
    gw, gw_send, gw_in, gq_send, gq_in, ar_own, ar_half, ar_slots, ar_total,
    local_sems, send_sems, recv_sems,
):
    c, f = lax.axis_index("ctx"), lax.axis_index("fsdp")
    y_hi, x, core = c // 8, (c // 2) % 4, c % 2
    z, y_lo = f // 2, f % 2
    y = 2 * y_hi + y_lo

    def at(x_at, y_at, z_at, core_at):
        return ((y_at // 2) * 8 + x_at * 2 + core_at, z_at * 2 + y_at % 2)

    def away(dx=0, dy=0, dz=0):
        return at((x + dx) % 4, (y + dy) % 4, (z + dz) % 4, core)

    sibling = (c + 1 - 2 * core, f)
    wire = Wire(send_sems, recv_sems)

    here = {"x": x, "y": y, "z": z}

    def by_core(w, of):
        first, second = (of(text) for text in ORDERS[w])
        return first + core * (second - first)

    def along(w, stage, k):
        return away(**{"d" + axis: k * by_core(w, lambda text: int(text[stage] == axis)) for axis in "xyz"})

    def place(w, stage):
        return by_core(w, lambda text: here[text[stage]])

    def final_target(w, i):
        return (4 * place(w, 0) + place(w, 1), 2 * place(w, 2) + i)

    def final_source(w, core_at):
        found = dict(zip(ORDERS[w][core_at], (c // 4, c % 4, f // 2)))
        return at(found["x"], found["y"], found["z"], core_at)

    own_rows = ds(f * SHARD, SHARD, SHARD)
    loads = []
    for j, ref in enumerate((w_query, w_key, w_value, w_out, w_up, w_down)):
        load = pltpu.make_async_copy(
            ref, shards.at[j] if j < 3 else weights.at[j - 3, own_rows], local_sems.at[j]
        )
        load.start()
        loads.append(load)

    barrier = pltpu.get_barrier_semaphore()
    peers = [((c + k) % 16, f) for k in range(1, 16)] + [(c, (f + k) % 8) for k in range(1, 8)]
    peers.append(at(x, 3 - y, z, core))
    for w in range(3):
        peers += [final_target(w, i) for i in range(2)] + [final_source(w, i) for i in range(2)]
    for peer in peers:
        pl.semaphore_signal(barrier, inc=1, device_id=peer, device_id_type=MESH)

    gain_one, gain_two = g_attn[...].reshape(1, D), g_mlp[...].reshape(1, D)
    bias_up, bias_down = b_up[...].reshape(1, D), b_down[...].reshape(1, D)
    x_in = tokens[...].astype(f32)
    r_one = lax.rsqrt(jnp.mean(x_in * x_in, axis=1, keepdims=True) + EPS)
    gathered[ds(c * BLK, BLK, BLK), :] = (x_in * r_one * gain_one).astype(bf16)
    scale = QUERY_CONST * jnp.log(1.0 + jnp.exp(q_scale[...].reshape(1, HEAD_DIM)))
    scale_col = jnp.broadcast_to(scale, (BLK, HEAD_DIM)).T[:, :1]

    from_col = lax.broadcasted_iota(jnp.int32, (D, 256), 0) - c * HEAD_DIM
    to_col = lax.broadcasted_iota(jnp.int32, (D, 256), 1)
    own_cols = jnp.zeros((SHARD, 256), f32)
    for j in range(3):
        loads[j].wait()
        pick = (from_col >= 0) & (from_col < HEAD_DIM) & (to_col == from_col + j * HEAD_DIM)
        own_cols = own_cols + nn(shards[j], jnp.where(pick, 1.0, 0.0).astype(bf16))
    wqkv_all[own_rows, :] = own_cols.astype(bf16)
    keep = pltpu.make_async_copy(shards, later_weights.at[:, own_rows], local_sems.at[6])
    keep.start()

    pl.semaphore_wait(barrier, len(peers))

    def piece(yh, xa, co, part=None):
        start = ((yh * 4 + xa) * 2 + co) * BLK
        if part is None:
            return gathered.at[ds(start, BLK, BLK)]
        return gathered.at[ds(start + part * 64, 64, 64)]

    other = 1 - y_hi
    xl, xr, xo = (x + 3) % 4, (x + 1) % 4, (x + 2) % 4
    def pass_chunk(yh, xa, part, device):
        chunk = piece(yh, xa, core, part)
        return wire.send(chunk, chunk, device)

    left, right, across = away(dx=3), away(dx=1), away(dy=2)
    to_y, to_xr, to_xl = {}, {}, {}
    def columns_at(zz, lo):
        return wqkv_all.at[ds((zz * 2 + lo) * SHARD, SHARD, SHARD)]

    def columns_round_z(lo):
        return [wire.send(columns_at(z, lo), columns_at(z, lo), away(dz=k)) for k in (1, 3, 2)]

    pair = (c, f + 1 - 2 * y_lo)
    for one, other_one in ((0, 1), (1, 0)):
        to_y[one] = pass_chunk(y_hi, x, one, across)
        to_xr[one] = pass_chunk(y_hi, x, one, right)
        to_xl[other_one] = pass_chunk(y_hi, x, other_one, left)
        if one == 0:
            cols_y = wire.send(columns_at(z, y_lo), columns_at(z, y_lo), pair)
    to_core = wire.send(piece(y_hi, x, core), piece(y_hi, x, core), sibling)
    cols_z = columns_round_z(y_lo)

    half_cols = ds(core * HALF, HALF, 128)
    across_y = (y + 1 + 2 * core) % 4
    from_y = (y + 3 + 2 * core) % 4

    def rows_of(view, zz, lo, first=0, count=SHARD):
        buffer, at_first, number = view
        return buffer.at[pl.ds(at_first, number), ds((zz * 2 + lo) * SHARD + first, count, 16), half_cols]

    zl, zr, zo = (z + 3) % 4, (z + 1) % 4, (z + 2) % 4

    class Gather:
        def __init__(self, buffer, own, split):
            self.buffer, self.own, self.split = buffer, own, split
            self.first, self.count, self.left = (80 * (x % 2), 80, 48) if split else (0, SHARD, 80)
            self.kept, self.over_x = [], []

        def rows(self, zz, lo, part=None):
            first, count = self.first, self.count
            if part is not None:
                first, count = (first, self.left) if part == 0 else (first + self.left, count - self.left)
            return rows_of(self.buffer, zz, lo, first, count)

        def begin(self):
            own, one = self.own(self.first, self.count), self.rows(z, y_lo)
            self.r0 = wire.send(own, one, away(dz=1))
            self.l0 = wire.send(own, one, away(dz=3))

        def begin_y(self):
            self.y = wire.send(self.own(self.first, self.count), self.rows(z, y_lo), at(x, across_y, z, core))

        def give(self, zz, lo):
            ref = self.rows(zz, lo)
            self.kept.append((wire.send(ref, ref, sibling), ref))
            if self.split:
                self.over_x.append((wire.send(ref, ref, at((x + 1 + 2 * core) % 4, y, z, core)), zz, lo))

        def second(self):
            two = self.rows(z, 1 - y_lo)
            wire.receive(self.y, two, at(x, from_y, z, core))
            self.r1 = wire.send(two, two, away(dz=1))
            self.l1 = wire.send(two, two, away(dz=3))
            self.give(z, 1 - y_lo)

        def forward(self, lo, left, right):
            wire.receive(right, self.rows(zl, lo), away(dz=3))
            one = self.rows(zl, lo, 0)
            to_right = wire.send(one, one, away(dz=1))
            wire.receive(left, self.rows(zr, lo), away(dz=1))
            two = self.rows(zr, lo, 1)
            to_left = wire.send(two, two, away(dz=3))
            self.give(zl, lo)
            self.give(zr, lo)
            return to_right, to_left

        def third(self):
            self.f0 = self.forward(y_lo, self.l0, self.r0)

        def fourth(self):
            self.f1 = self.forward(1 - y_lo, self.l1, self.r1)

        def last(self, lo, pair):
            wire.receive(pair[0], self.rows(zo, lo, 0), away(dz=3))
            wire.receive(pair[1], self.rows(zo, lo, 1), away(dz=1))
            self.give(zo, lo)

        def fifth(self):
            self.last(y_lo, self.f0)

        def sixth(self):
            self.last(1 - y_lo, self.f1)

        def seventh(self):
            for index, zz, lo in self.over_x:
                ref = rows_of(self.buffer, zz, lo, 80 - self.first, 80)
                wire.receive(index, ref, at((x + 3 + 2 * core) % 4, y, z, core))
                self.kept.append((wire.send(ref, ref, sibling), ref))

        def finish(self):
            for index, ref in self.kept:
                wire.receive(index, ref, sibling)

    def early(j, split):
        view = (weights, j, 1)
        return Gather(view, lambda first, count: rows_of(view, z, y_lo, first, count), split)

    out_rows, up_rows, down_rows = early(0, False), early(1, True), early(2, True)
    second_set = Gather((later_weights, 0, 3), lambda first, count: shards.at[:, ds(first, count, 16), half_cols], True)
    for load in loads[3:]:
        load.wait()
    out_rows.begin()

    def project(yh, xa):
        chip = yh * 4 + xa
        both = nt(wqkv_t[...], gathered[ds(chip * TILE, TILE, TILE), :])
        for i in range(2):
            one = both[:, i * BLK:(i + 1) * BLK]
            raw_q[2 * chip + i] = one[:HEAD_DIM]
            qkv_slot[2 * chip + i, :HEAD_DIM] = (one[:HEAD_DIM] * scale_col).astype(bf16)
            qkv_slot[2 * chip + i, HEAD_DIM:] = one[HEAD_DIM:240].astype(bf16)

    def take(indices, yh, xa, device, parts=(0, 1)):
        for part in parts:
            wire.receive(indices[part], piece(yh, xa, core, part), device)

    def to_sibling(yh, xa):
        return wire.send(piece(yh, xa, core), piece(yh, xa, core), sibling)

    def both_cores(index, yh, xa):
        wire.receive(index, piece(yh, xa, 1 - core), sibling)
        project(yh, xa)

    wire.receive(cols_y, columns_at(z, 1 - y_lo), pair)
    cols_yz = columns_round_z(1 - y_lo)
    down_rows.begin()
    up_rows.begin()
    ring, y_r, y_l = {}, {}, {}
    take(to_xr, y_hi, xl, left, (0,))
    ring[0] = pass_chunk(y_hi, xl, 0, right)
    take(to_xl, y_hi, xr, right, (1,))
    ring[1] = pass_chunk(y_hi, xr, 1, left)
    take(to_y, other, x, across, (0,))
    y_r[0] = pass_chunk(other, x, 0, right)
    y_l[0] = pass_chunk(other, x, 0, left)
    take(to_xr, y_hi, xl, left, (1,))
    core_l = to_sibling(y_hi, xl)
    take(to_xl, y_hi, xr, right, (0,))
    core_r = to_sibling(y_hi, xr)
    take(to_y, other, x, across, (1,))
    y_r[1] = pass_chunk(other, x, 1, right)
    y_l[1] = pass_chunk(other, x, 1, left)
    core_y = to_sibling(other, x)
    out_rows.begin_y()
    down_rows.begin_y()
    up_rows.begin_y()
    for index, k in zip(cols_z, (1, 3, 2)):
        wire.receive(index, columns_at((z + 4 - k) % 4, y_lo), away(dz=4 - k))
    for index, k in zip(cols_yz, (1, 3, 2)):
        wire.receive(index, columns_at((z + 4 - k) % 4, 1 - y_lo), away(dz=4 - k))
    wqkv_t[...] = flip(wqkv_all[...])
    far = {}
    wire.receive(ring[0], piece(y_hi, xo, core, 0), left)
    far[0] = pass_chunk(y_hi, xo, 0, across)
    wire.receive(ring[1], piece(y_hi, xo, core, 1), right)
    far[1] = pass_chunk(y_hi, xo, 1, across)
    core_o = to_sibling(y_hi, xo)
    out_rows.third()
    both_cores(to_core, y_hi, x)
    both_cores(core_l, y_hi, xl)
    both_cores(core_r, y_hi, xr)
    out_rows.second()
    both_cores(core_y, other, x)
    take(y_r, other, xl, left)
    core_yl = to_sibling(other, xl)
    take(y_l, other, xr, right)
    core_yr = to_sibling(other, xr)
    down_rows.second()
    up_rows.second()
    both_cores(core_o, y_hi, xo)
    down_rows.third()
    up_rows.third()
    both_cores(core_yl, other, xl)
    both_cores(core_yr, other, xr)
    take(far, other, xo, across)
    core_f = to_sibling(other, xo)
    out_rows.fourth()
    both_cores(core_f, other, xo)

    waiting = [
        down_rows.fourth, up_rows.fourth, out_rows.fifth, second_set.begin_y, second_set.begin,
        down_rows.fifth, up_rows.fifth, out_rows.sixth, down_rows.sixth, up_rows.sixth,
    ]

    def move_on(number):
        for _ in range(number):
            if waiting:
                waiting.pop(0)()

    slot_of = []
    for p in range(NBLK):
        slot = 0
        for b in range(NBLK):
            slot = jnp.where(order[0, b] == p, b, slot)
        slot_of.append(slot)
    for p in range(NBLK):
        qkv_pos[:, p * BLK:(p + 1) * BLK] = qkv_slot[slot_of[p]]
        raw_pos[:, p * BLK:(p + 1) * BLK] = raw_q[slot_of[p]]
    k_rows[...] = flip(qkv_pos[HEAD_DIM:2 * HEAD_DIM, :])
    v_rows[...] = flip(qkv_pos[2 * HEAD_DIM:, :])

    ends, total = [], 0
    for s in range(4):
        total = total + lengths[0, s]
        ends.append(total)

    at_part = 0
    parts_of = []
    for t in range(GROUP // TILE):
        low, high = max(0, t * TILE - WINDOW), (t + 1) * TILE
        width = high - low
        tile = slice(t * TILE, high)
        scores = nn(k_rows[low:high, :], qkv_pos[:HEAD_DIM, tile])
        at_q = t * TILE + lax.broadcasted_iota(jnp.int32, (1, TILE), 1)
        start = jnp.zeros((1, TILE), jnp.int32)
        for end in ends:
            start = jnp.where(at_q >= end, end, start)
        at_k = low + lax.broadcasted_iota(jnp.int32, (width, TILE), 0)
        scores = jnp.where((at_k <= at_q) & (at_k >= start), scores, MASKED)
        top = jnp.max(scores, axis=0, keepdims=True)
        powers = jnp.exp(scores - top)
        part = powers * (1.0 / jnp.sum(powers, axis=0, keepdims=True))
        part = part.astype(bf16)
        parts_of.append(slice(at_part, at_part + width))
        at_part += width
        probs[parts_of[t], :] = part
        out = nn(qkv_pos[2 * HEAD_DIM:, low:high], part).astype(bf16)
        out_pos[2 * t] = out[:, :BLK]
        out_pos[2 * t + 1] = out[:, BLK:]
        move_on(1)

    for b in range(NBLK):
        head_send[b] = out_pos[order[0, b]]

    def exchange(src_of, dst):
        return [wire.send(src_of((c + k) % 16), dst, ((c + k) % 16, f)) for k in range(1, 16)]

    def arrive(indices, dst_of):
        for k, index in enumerate(indices):
            src = (c + 15 - k) % 16
            wire.receive(index, dst_of(src), (src, f))

    head_rows = ds(c * HEAD_DIM, HEAD_DIM, HEAD_DIM)
    mixing = exchange(lambda b: head_send.at[b], mixed_t.at[head_rows])
    mixed_t[head_rows, :] = head_send[c]
    move_on(len(waiting))
    second_set.second()

    cot_f = cot[...].astype(f32)

    def spread(a, w):
        return jnp.concatenate([nn(a, weights[w, :, n:n + 256]) for n in range(0, D, 256)], axis=1)

    def spread_back(a, w):
        return jnp.concatenate([nt(a, weights[w, n:n + 256, :]) for n in range(0, D, 256)], axis=1)

    out_rows.finish()
    arrive(mixing, lambda src: mixed_t.at[ds(src * HEAD_DIM, HEAD_DIM, HEAD_DIM)])

    my_lanes, sib_lanes = ds(core * BLK, BLK, BLK), ds((1 - core) * BLK, BLK, BLK)
    other_half = ds((1 - core) * HALF, HALF, 128)

    def share(w, rows_t, up):
        acts[w, :, my_lanes] = rows_t
        up_in[w] = up
        indices = (
            wire.send(acts.at[w, :, my_lanes], acts.at[w, :, my_lanes], sibling),
            wire.send(up_in.at[w, :, other_half], up_all.at[w, my_lanes], sibling),
        )
        up_all[w, my_lanes, :] = up_in[w, :, half_cols]
        return indices

    mixed = flip(mixed_t[...])
    after = x_in + spread(mixed, 0)
    r_two = lax.rsqrt(jnp.mean(after * after, axis=1, keepdims=True) + EPS)
    n_two = after * r_two
    normed_two = (n_two * gain_two).astype(bf16)
    up_rows.seventh()
    down_rows.seventh()
    up_rows.finish()
    hidden = spread(normed_two, 1) + bias_up
    gate = jax.nn.sigmoid(hidden)
    active = (hidden * gate).astype(bf16)
    shared = {2: share(2, flip(active), cot[...])}
    down_rows.finish()
    wire.set_one = len(wire.sent)
    grad_active = spread_back(cot[...], 2)
    grad_hidden = (grad_active * gate * (1.0 + hidden * (1.0 - gate))).astype(bf16)
    shared[1] = share(1, flip(normed_two), grad_hidden)
    back_two = spread_back(grad_hidden, 1)
    scaled = back_two * gain_two
    grad_after = cot_f + r_two * (scaled - n_two * jnp.mean(scaled * n_two, axis=1, keepdims=True))
    grad_branch = grad_after.astype(bf16)
    dout_t[...] = flip(spread_back(grad_branch, 0).astype(bf16))
    douts = exchange(lambda b: dout_t.at[ds(b * HEAD_DIM, HEAD_DIM, HEAD_DIM)], dout_slot.at[c])
    dout_slot[c] = dout_t[head_rows, :]
    shared[0] = share(0, mixed_t[...], grad_branch)

    second_set.third()
    def scatter(w, stage, src_of, dst_of):
        return [wire.send(src_of((place(w, stage) + k) % 4), dst_of(k - 1), along(w, stage, k)) for k in range(1, 4)]

    def gathered_sum(w, stage, indices, first, buffers):
        for k, index in enumerate(indices):
            wire.receive(index, buffers.at[w, k], along(w, stage, 3 - k))
        return first.astype(f32) + buffers[w, 0].astype(f32) + buffers[w, 1].astype(f32) + buffers[w, 2].astype(f32)

    stage_one, stage_two, stage_three = {}, {}, {}
    for w in (2, 1, 0):
        wire.receive(shared[w][0], acts.at[w, :, sib_lanes], sibling)
        wire.receive(shared[w][1], up_all.at[w, sib_lanes], sibling)
        for n in range(0, D, 320):
            rows = slice(n, n + 320)
            t1[w, rows, :] = nn(acts[w, rows, :], up_all[w]).astype(bf16)
        stage_one[w] = scatter(w, 0, lambda d: t1.at[w, ds(d * 320, 320, 320)], lambda k: r1.at[w, k])

    layer_out[...] = (after + spread(active, 2) + bias_down).astype(bf16)
    input_grad[...] = grad_after
    ar_own[...] = jnp.zeros_like(ar_own)
    ar_own[1:2, :] = jnp.sum(back_two * n_two, axis=0, keepdims=True)
    ar_own[2:3, :] = jnp.sum(grad_hidden.astype(f32), axis=0, keepdims=True)
    ar_own[3:4, :] = jnp.sum(cot_f, axis=0, keepdims=True)
    def second_stage(w):
        mine = t1[w, ds(place(w, 0) * 320, 320, 320), :]
        t2[w] = gathered_sum(w, 0, stage_one[w], mine, r1).astype(bf16)
        stage_two[w] = scatter(w, 1, lambda d: t2.at[w, ds(d * 80, 80, 80)], lambda k: r2.at[w, k])

    def third_stage(w):
        mine = t2[w, ds(place(w, 1) * 80, 80, 80), :]
        both = gathered_sum(w, 1, stage_two[w], mine, r2)
        for d in range(4):
            t3[w, d] = jnp.concatenate([both[20 * d:20 * d + 20], jnp.zeros((12, HALF), f32)], axis=0).astype(bf16)
        stage_three[w] = scatter(w, 2, lambda d: t3.at[w, d], lambda k: r3.at[w, k])

    def fourth_stage(w):
        both = gathered_sum(w, 2, stage_three[w], t3[w, place(w, 2)], r3)
        base = wire.used
        wire.used += 2
        copies = []
        for i in range(2):
            rows_out[w, i] = jnp.concatenate([both[10 * i:10 * i + 10], jnp.zeros((6, HALF), f32)], axis=0)
            target = final_target(w, i)
            stays = (target[0] == c) & (target[1] == f)
            to = rows_in.at[w, :, half_cols]
            copy = pltpu.make_async_remote_copy(
                src_ref=rows_out.at[w, i], dst_ref=to, send_sem=send_sems.at[base + i],
                recv_sem=recv_sems.at[base + core], device_id=target, device_id_type=MESH,
            )
            within = pltpu.make_async_copy(rows_out.at[w, i], to, recv_sems.at[base + core])
            pl.when(jnp.logical_not(stays))(copy.start)
            pl.when(stays)(within.start)
            copies.append((copy, stays))
        return w, base, copies

    second_set.fourth()
    arrive(douts, lambda src: dout_slot.at[src])

    for p in range(NBLK):
        dout_pos[:, p * BLK:(p + 1) * BLK] = dout_slot[slot_of[p]]
    dk_acc[...] = jnp.zeros_like(dk_acc)
    dv_acc[...] = jnp.zeros_like(dv_acc)
    scale_terms = jnp.zeros((HEAD_DIM, 1), f32)
    for t in range(GROUP // TILE):
        low, high = max(0, t * TILE - WINDOW), (t + 1) * TILE
        width = high - low
        tile = slice(t * TILE, high)
        d_out = dout_pos[:, tile]
        delta = jnp.sum(d_out.astype(f32) * jnp.concatenate([out_pos[2 * t], out_pos[2 * t + 1]], axis=1).astype(f32), axis=0, keepdims=True)
        part = probs[parts_of[t], :]
        d_probs = nn(v_rows[low:high, :], d_out)
        d_scores = (part.astype(f32) * (d_probs - delta)).astype(bf16)
        dq = nn(qkv_pos[HEAD_DIM:2 * HEAD_DIM, low:high], d_scores)
        scale_terms = scale_terms + jnp.sum(dq * raw_pos[:, tile], axis=1, keepdims=True)
        dq = (dq * scale_col).astype(bf16)
        grads_pos[2 * t, :HEAD_DIM] = dq[:, :BLK]
        grads_pos[2 * t + 1, :HEAD_DIM] = dq[:, BLK:]
        if t in (3, 6):
            (second_set.fifth, second_set.sixth)[t // 4]()
        dk_acc[:, low:high] += nt(qkv_pos[:HEAD_DIM, tile], d_scores)
        dv_acc[:, low:high] += nt(d_out, part)

    for p in range(NBLK):
        lanes = slice(p * BLK, (p + 1) * BLK)
        grads_pos[p, HEAD_DIM:2 * HEAD_DIM] = dk_acc[:, lanes].astype(bf16)
        grads_pos[p, 2 * HEAD_DIM:] = dv_acc[:, lanes].astype(bf16)
    for b in range(NBLK):
        block = grads_pos[order[0, b]]
        qkv_slot[b] = block
        grads_flat[:, b * BLK:(b + 1) * BLK] = block
    sent_grads = exchange(lambda b: qkv_slot.at[b], grads_in.at[c])
    grads_in[c] = qkv_slot[c]

    for n in range(0, D, 256):
        grad_t = nn(grads_flat[...], gathered[:, n:n + 256])
        by_gain = jnp.sum(wqkv_t[:240, n:n + 256].astype(f32) * grad_t, axis=0, keepdims=True)
        ar_own[0:1, n:n + 256] = by_gain / gain_one[:, n:n + 256]
        gw[n:n + 256, :] = jnp.concatenate([grad_t, jnp.zeros((16, 256), f32)], axis=0).T
    for fs in range(8):
        picked = [gw[cs * 80 + fs * 10:cs * 80 + fs * 10 + 10, :] for cs in range(16)]
        gw_send[fs] = jnp.concatenate(picked, axis=0).astype(bf16)
    ar_own[4:5, :HEAD_DIM] = jnp.broadcast_to(scale_terms, (HEAD_DIM, BLK)).T[:1]
    half_sums = wire.send(ar_own.at[:, other_half], ar_half, sibling)
    shares = [wire.send(gw_send.at[(f + k) % 8], gw_in.at[k - 1], (c, (f + k) % 8)) for k in range(1, 8)]

    def spread_sums(i, axis, value):
        me = here[axis]
        ar_slots[i, me] = value
        return [wire.send(ar_slots.at[i, me], ar_slots.at[i, me], away(**{"d" + axis: k})) for k in range(1, 4)]

    def collect_sums(i, axis, indices):
        for k, index in enumerate(indices):
            wire.receive(index, ar_slots.at[i, (here[axis] + 3 - k) % 4], away(**{"d" + axis: 3 - k}))
        return ar_slots[i, 0] + ar_slots[i, 1] + ar_slots[i, 2] + ar_slots[i, 3]

    wire.receive(half_sums, ar_half, sibling)
    sums = spread_sums(0, "x", ar_own[:, half_cols] + ar_half[...])
    second_set.seventh()
    second_stage(2)
    sums = spread_sums(1, "y", collect_sums(0, "x", sums))
    second_stage(1)
    second_stage(0)
    sums = spread_sums(2, "z", collect_sums(1, "y", sums))

    for k, index in enumerate(shares):
        src_f = (f + 7 - k) % 8
        wire.receive(index, gw_in.at[k], (c, src_f))
    both = gw_send[f].astype(f32)
    for k in range(7):
        both = both + gw_in[k].astype(f32)
    for cs in range(16):
        gq_send[cs] = jnp.concatenate([both[10 * cs:10 * cs + 10], jnp.zeros((6, 256), f32)], axis=0).astype(bf16)
    gq_in[c] = gq_send[c]
    heads = exchange(lambda b: gq_send.at[b], gq_in.at[c])
    third_stage(2)
    third_stage(1)
    third_stage(0)
    ar_total[:, half_cols] = collect_sums(2, "z", sums)
    half_sums = wire.send(ar_total.at[:, half_cols], ar_total.at[:, half_cols], sibling)

    second_set.finish()
    for copy in wire.sent[:wire.set_one]:
        copy.wait_send()
    wire.sent = wire.sent[wire.set_one:]
    keep.wait()
    loads = []
    for j in range(3):
        load = pltpu.make_async_copy(later_weights.at[j], weights.at[j], local_sems.at[j])
        load.start()
        loads.append(load)
    arrive(sent_grads, lambda src: grads_in.at[src])
    grad_normed = jnp.zeros((BLK, D), f32)
    for j in range(3):
        loads[j].wait()
        rows = slice(j * HEAD_DIM, (j + 1) * HEAD_DIM)
        joined = jnp.concatenate([grads_in[h, rows] for h in range(HEADS)], axis=0)
        grad_normed = grad_normed + spread_back(flip(joined), j)
    n_one = x_in * r_one
    scaled = grad_normed * gain_one
    through = r_one * (scaled - n_one * jnp.mean(scaled * n_one, axis=1, keepdims=True))
    input_grad[...] = input_grad[...] + through

    finals = [fourth_stage(w) for w in (2, 1, 0)]

    wire.receive(half_sums, ar_total.at[:, other_half], sibling)
    small_out[...] = ar_total[...]
    arrive(heads, lambda src: gq_in.at[src])
    grad_qkv[...] = gq_in[...]
    for w, base, copies in finals:
        for core_at in range(2):
            wire.receive(base + core_at, rows_in.at[w, :, core_at * HALF:(core_at + 1) * HALF], final_source(w, core_at))
        for copy, stays in copies:
            pl.when(jnp.logical_not(stays))(copy.wait_send)
    grad_mlp[...] = rows_in[...]
    wire.drain()
    assert wire.used <= N_SEM


def outputs(
    out, in_grad, rows, qkv, small, q_scale,
    layer_out, input_grad, g_query, g_key, g_value, g_out, g_up, g_down, g_gain_one, g_gain_two, g_scale, g_bias_up, g_bias_down,
    rows_here, qkv_here, small_here, sems,
):
    places = (layer_out.at[0], input_grad.at[0], rows_here, qkv_here, small_here)
    copies = [
        pltpu.make_async_copy(src, dst, sems.at[i]) for i, (src, dst) in enumerate(zip((out, in_grad, rows, qkv, small), places))
    ]
    for copy in copies:
        copy.start()
    for copy in copies:
        copy.wait()
    rows, qkv, small = rows_here, qkv_here, small_here
    for j, ref in enumerate((g_query, g_key, g_value)):
        tiles = [jnp.zeros((16, BLK), f32) for _ in range(11)]
        for h in range(HEADS):
            tile, start = divmod(h * HEAD_DIM, BLK)
            moved = pltpu.roll(qkv[h].astype(f32), (start - j * HEAD_DIM) % 256, 1)
            lane = lax.broadcasted_iota(jnp.int32, (16, 256), 1)
            moved = jnp.where((lane >= start) & (lane < start + HEAD_DIM), moved, 0.0)
            tiles[tile] = tiles[tile] + moved[:, :BLK]
            tiles[tile + 1] = tiles[tile + 1] + moved[:, BLK:]
        ref[...] = jnp.concatenate(tiles[:10], axis=1)[:10]
    for w, ref in enumerate((g_out, g_up, g_down)):
        ref[...] = rows[w, :10, :]
    for i, ref in ((0, g_gain_one), (1, g_gain_two), (2, g_bias_up), (3, g_bias_down)):
        ref[...] = small[i, :]
    g_scale[...] = small[4, :HEAD_DIM] * QUERY_CONST * jax.nn.sigmoid(q_scale[...])


def on_device(
    tokens, cotangent, lengths, block_order, w_query, w_key, w_value, w_out, w_up, w_down,
    g_attn, g_mlp, q_scale, b_up, b_down,
):
    vmem, smem, any_space = (pl.BlockSpec(memory_space=s) for s in (pltpu.VMEM, pltpu.SMEM, pl.ANY))
    shapes = {
        "weights": ((3, D, D), bf16), "shards": ((3, SHARD, D), bf16), "gathered": ((GROUP, D), bf16), "wqkv_all": ((D, 256), bf16),
        "wqkv_t": ((256, D), bf16), "raw_q": ((NBLK, HEAD_DIM, BLK), f32), "qkv_slot": ((NBLK, 240, BLK), bf16),
        "qkv_pos": ((240, GROUP), bf16), "raw_pos": ((HEAD_DIM, GROUP), f32), "k_rows": ((GROUP, HEAD_DIM), bf16),
        "v_rows": ((GROUP, HEAD_DIM), bf16), "probs": ((7680, TILE), bf16), "out_pos": ((NBLK, HEAD_DIM, BLK), bf16),
        "head_send": ((NBLK, HEAD_DIM, BLK), bf16), "mixed_t": ((D, BLK), bf16), "dout_t": ((D, BLK), bf16),
        "dout_slot": ((NBLK, HEAD_DIM, BLK), bf16), "dout_pos": ((HEAD_DIM, GROUP), bf16),
        "dk_acc": ((HEAD_DIM, GROUP), f32), "dv_acc": ((HEAD_DIM, GROUP), f32), "grads_pos": ((NBLK, 240, BLK), bf16),
        "grads_flat": ((240, GROUP), bf16), "grads_in": ((NBLK, 240, BLK), bf16),
        "acts": ((3, D, 2 * BLK), bf16), "up_in": ((3, BLK, D), bf16), "up_all": ((3, 2 * BLK, HALF), bf16),
        "t1": ((3, D, HALF), bf16), "r1": ((3, 3, 320, HALF), bf16), "t2": ((3, 320, HALF), bf16),
        "r2": ((3, 3, 80, HALF), bf16), "t3": ((3, 4, 32, HALF), bf16), "r3": ((3, 3, 32, HALF), bf16),
        "rows_out": ((3, 2, 16, HALF), f32), "rows_in": ((3, 16, D), f32),
        "gw": ((D, 256), f32), "gw_send": ((8, SHARD, 256), bf16), "gw_in": ((7, SHARD, 256), bf16),
        "gq_send": ((16, 16, 256), bf16), "gq_in": ((16, 16, 256), bf16),
        "ar_own": ((8, D), f32), "ar_half": ((8, HALF), f32), "ar_slots": ((3, 4, 8, HALF), f32),
        "ar_total": ((8, D), f32),
    }
    outs = {
        "layer_out": ((BLK, D), bf16), "input_grad": ((BLK, D), f32), "grad_mlp": ((3, 16, D), f32),
        "grad_qkv": ((16, 16, 256), bf16), "small_out": ((8, D), f32), "later_weights": ((3, D, D), bf16),
    }
    ins = (
        "lengths", "order", "tokens", "cot", "w_out", "w_up", "w_down", "w_query", "w_key", "w_value",
        "g_attn", "g_mlp", "q_scale", "b_up", "b_down",
    )

    def body(*refs):
        names = ins + tuple(outs) + tuple(shapes) + ("local_sems", "send_sems", "recv_sems")
        layer(**dict(zip(names, refs, strict=True)))

    out, in_grad, rows, qkv, small, _ = pl.pallas_call(
        body,
        out_shape=[jax.ShapeDtypeStruct(*s) for s in outs.values()],
        in_specs=[smem, smem] + [vmem] * 2 + [any_space] * 6 + [vmem] * 5,
        out_specs=[vmem] * (len(outs) - 1) + [any_space],
        scratch_shapes=[pltpu.VMEM(*s) for s in shapes.values()]
        + [pltpu.SemaphoreType.DMA((7,)), pltpu.SemaphoreType.DMA((N_SEM,)), pltpu.SemaphoreType.DMA((N_SEM,))],
        compiler_params=pltpu.CompilerParams(
            collective_id=0, has_side_effects=True, vmem_limit_bytes=62 << 20
        ),
    )(
        lengths, block_order, tokens[0], cotangent[0], w_out, w_up, w_down, w_query, w_key, w_value,
        g_attn, g_mlp, q_scale, b_up, b_down,
    )
    row = jax.ShapeDtypeStruct((10, D), f32)
    vector = jax.ShapeDtypeStruct((D,), f32)
    return pl.pallas_call(
        outputs,
        out_shape=[
            jax.ShapeDtypeStruct((1, BLK, D), bf16), jax.ShapeDtypeStruct((1, BLK, D), f32), *[row] * 6,
            vector, vector, jax.ShapeDtypeStruct((HEAD_DIM,), f32), vector, vector,
        ],
        in_specs=[any_space] * 5 + [vmem],
        out_specs=[vmem] * 13,
        scratch_shapes=[
            pltpu.VMEM((3, 16, D), f32), pltpu.VMEM((16, 16, 256), bf16), pltpu.VMEM((8, D), f32),
            pltpu.SemaphoreType.DMA((5,)),
        ],
        compiler_params=pltpu.CompilerParams(vmem_limit_bytes=62 << 20),
    )(out, in_grad, rows, qkv, small, q_scale)


def solution(mesh):
    tokens, rows, whole = P("fsdp", "ctx", None), P("fsdp", None), P()
    owned = P(("ctx", "fsdp"), None)
    return jax.shard_map(
        on_device, mesh=mesh,
        in_specs=(tokens, tokens, rows, rows) + (rows,) * 6 + (whole,) * 5,
        out_specs=(tokens, tokens) + (owned,) * 6 + (whole,) * 5,
        check_vma=False,
    )
```

```python
import functools
import math

import jax
import jax.numpy as jnp
from jax import lax
from jax.experimental import pallas as pl
from jax.experimental.pallas import tpu as pltpu
from jax.sharding import PartitionSpec as P

D = 1280
HEADS = 16
HEAD_DIM = 80
BLK = 128
GROUP = 2048
NBLK = 16
SHARD = 160
HALF = 640
TILE = 256
WINDOW = 1024
EPS = 1e-06
QUERY_CONST = 1.442695 / math.sqrt(HEAD_DIM)
MASKED = -1e30
N_SEM = 288
ORDERS = (("yxz", "yxz"), ("xzy", "xzy"), ("zyx", "zyx"))
MESH = pl.DeviceIdType.MESH
bf16, f32 = jnp.bfloat16, jnp.float32


def nn(a, b):
    return jnp.dot(a, b, preferred_element_type=f32)


def nt(a, b):
    return lax.dot_general(a, b, (((1,), (1,)), ((), ())), preferred_element_type=f32)


def ds(start, size, unit):
    return pl.ds(pl.multiple_of(start, unit), size)


def flip(matrix):
    return matrix.astype(f32).T.astype(matrix.dtype)


class Wire:
    def __init__(self, send_sems, recv_sems):
        self.send_sems, self.recv_sems, self.used, self.sent = send_sems, recv_sems, 0, []

    def copy(self, index, src, dst, device):
        return pltpu.make_async_remote_copy(
            src_ref=src, dst_ref=dst, send_sem=self.send_sems.at[index], recv_sem=self.recv_sems.at[index],
            device_id=device, device_id_type=MESH,
        )

    def send(self, src, dst, device):
        index = self.used
        self.used += 1
        copy = self.copy(index, src, dst, device)
        copy.start()
        self.sent.append(copy)
        return index

    def receive(self, index, ref, device):
        self.copy(index, ref, ref, device).wait_recv()

    def drain(self):
        for copy in self.sent:
            copy.wait_send()
        self.sent = []


def layer(
    lengths, order, tokens, cot, w_out, w_up, w_down, w_query, w_key, w_value,
    g_attn, g_mlp, q_scale, b_up, b_down,
    layer_out, input_grad, grad_mlp, grad_qkv, small_out,
    later_weights,
    weights, shards, gathered, wqkv_all, wqkv_t, raw_q, qkv_slot, qkv_pos, raw_pos, k_rows, v_rows, probs, out_pos,
    head_send, mixed_t, dout_t, dout_slot, dout_pos, dk_acc, dv_acc, grads_pos, grads_flat, grads_in,
    acts, up_in, up_all, t1, r1, t2, r2, t3, r3, rows_out, rows_in,
    gw, gw_send, gw_in, gq_send, gq_in, ar_own, ar_half, ar_slots, ar_total,
    layer_here, grad_here, local_sems, send_sems, recv_sems,
):
    c, f = lax.axis_index("ctx"), lax.axis_index("fsdp")
    y_hi, x, core = c // 8, (c // 2) % 4, c % 2
    z, y_lo = f // 2, f % 2
    y = 2 * y_hi + y_lo

    def at(x_at, y_at, z_at, core_at):
        return ((y_at // 2) * 8 + x_at * 2 + core_at, z_at * 2 + y_at % 2)

    def away(dx=0, dy=0, dz=0):
        return at((x + dx) % 4, (y + dy) % 4, (z + dz) % 4, core)

    sibling = (c + 1 - 2 * core, f)
    wire = Wire(send_sems, recv_sems)

    here = {"x": x, "y": y, "z": z}

    def by_core(w, of):
        first, second = (of(text) for text in ORDERS[w])
        return first + core * (second - first)

    def along(w, stage, k):
        return away(**{"d" + axis: k * by_core(w, lambda text: int(text[stage] == axis)) for axis in "xyz"})

    def place(w, stage):
        return by_core(w, lambda text: here[text[stage]])

    def final_target(w, i):
        return (4 * place(w, 0) + place(w, 1), 2 * place(w, 2) + i)

    def final_source(w, core_at):
        found = dict(zip(ORDERS[w][core_at], (c // 4, c % 4, f // 2)))
        return at(found["x"], found["y"], found["z"], core_at)

    own_rows = ds(f * SHARD, SHARD, SHARD)
    loads = []
    for j, ref in enumerate((w_query, w_key, w_value, w_out, w_up, w_down)):
        load = pltpu.make_async_copy(
            ref, shards.at[j] if j < 3 else weights.at[j - 3, own_rows], local_sems.at[j]
        )
        load.start()
        loads.append(load)

    barrier = pltpu.get_barrier_semaphore()
    peers = [((c + k) % 16, f) for k in range(1, 16)] + [(c, (f + k) % 8) for k in range(1, 8)]
    peers.append(at(x, 3 - y, z, core))
    for w in range(3):
        peers += [final_target(w, i) for i in range(2)] + [final_source(w, i) for i in range(2)]
    for peer in peers:
        pl.semaphore_signal(barrier, inc=1, device_id=peer, device_id_type=MESH)

    gain_one, gain_two = g_attn[...].reshape(1, D), g_mlp[...].reshape(1, D)
    bias_up, bias_down = b_up[...].reshape(1, D), b_down[...].reshape(1, D)
    x_in = tokens[...].astype(f32)
    r_one = lax.rsqrt(jnp.mean(x_in * x_in, axis=1, keepdims=True) + EPS)
    gathered[ds(c * BLK, BLK, BLK), :] = (x_in * r_one * gain_one).astype(bf16)
    scale = QUERY_CONST * jnp.log(1.0 + jnp.exp(q_scale[...].reshape(1, HEAD_DIM)))
    scale_col = jnp.broadcast_to(scale, (BLK, HEAD_DIM)).T[:, :1]

    from_col = lax.broadcasted_iota(jnp.int32, (D, 256), 0) - c * HEAD_DIM
    to_col = lax.broadcasted_iota(jnp.int32, (D, 256), 1)
    own_cols = jnp.zeros((SHARD, 256), f32)
    for j in range(3):
        loads[j].wait()
        pick = (from_col >= 0) & (from_col < HEAD_DIM) & (to_col == from_col + j * HEAD_DIM)
        own_cols = own_cols + nn(shards[j], jnp.where(pick, 1.0, 0.0).astype(bf16))
    wqkv_all[own_rows, :] = own_cols.astype(bf16)
    keep = pltpu.make_async_copy(shards, later_weights.at[:, own_rows], local_sems.at[6])
    keep.start()

    pl.semaphore_wait(barrier, len(peers))

    def piece(yh, xa, co, part=None):
        start = ((yh * 4 + xa) * 2 + co) * BLK
        if part is None:
            return gathered.at[ds(start, BLK, BLK)]
        return gathered.at[ds(start + part * 64, 64, 64)]

    other = 1 - y_hi
    xl, xr, xo = (x + 3) % 4, (x + 1) % 4, (x + 2) % 4
    def pass_chunk(yh, xa, part, device):
        chunk = piece(yh, xa, core, part)
        return wire.send(chunk, chunk, device)

    left, right, across = away(dx=3), away(dx=1), away(dy=2)
    to_y, to_xr, to_xl = {}, {}, {}
    def columns_at(zz, lo):
        return wqkv_all.at[ds((zz * 2 + lo) * SHARD, SHARD, SHARD)]

    def columns_round_z(lo):
        return [wire.send(columns_at(z, lo), columns_at(z, lo), away(dz=k)) for k in (1, 3, 2)]

    pair = (c, f + 1 - 2 * y_lo)
    for one, other_one in ((0, 1), (1, 0)):
        to_y[one] = pass_chunk(y_hi, x, one, across)
        to_xr[one] = pass_chunk(y_hi, x, one, right)
        to_xl[other_one] = pass_chunk(y_hi, x, other_one, left)
        if one == 0:
            cols_y = wire.send(columns_at(z, y_lo), columns_at(z, y_lo), pair)
    to_core = wire.send(piece(y_hi, x, core), piece(y_hi, x, core), sibling)
    cols_z = columns_round_z(y_lo)

    half_cols = ds(core * HALF, HALF, 128)
    across_y = (y + 1 + 2 * core) % 4
    from_y = (y + 3 + 2 * core) % 4

    def rows_of(view, zz, lo, first=0, count=SHARD):
        buffer, at_first, number = view
        return buffer.at[pl.ds(at_first, number), ds((zz * 2 + lo) * SHARD + first, count, 16), half_cols]

    zl, zr, zo = (z + 3) % 4, (z + 1) % 4, (z + 2) % 4

    class Gather:
        def __init__(self, buffer, own, split):
            self.buffer, self.own, self.split = buffer, own, split
            self.first, self.count, self.left = (80 * (x % 2), 80, 48) if split else (0, SHARD, 80)
            self.kept, self.over_x = [], []

        def rows(self, zz, lo, part=None):
            first, count = self.first, self.count
            if part is not None:
                first, count = (first, self.left) if part == 0 else (first + self.left, count - self.left)
            return rows_of(self.buffer, zz, lo, first, count)

        def begin(self):
            own, one = self.own(self.first, self.count), self.rows(z, y_lo)
            self.r0 = wire.send(own, one, away(dz=1))
            self.l0 = wire.send(own, one, away(dz=3))

        def begin_y(self):
            self.y = wire.send(self.own(self.first, self.count), self.rows(z, y_lo), at(x, across_y, z, core))

        def give(self, zz, lo):
            ref = self.rows(zz, lo)
            self.kept.append((wire.send(ref, ref, sibling), ref))
            if self.split:
                self.over_x.append((wire.send(ref, ref, at((x + 1 + 2 * core) % 4, y, z, core)), zz, lo))

        def second(self):
            two = self.rows(z, 1 - y_lo)
            wire.receive(self.y, two, at(x, from_y, z, core))
            self.r1 = wire.send(two, two, away(dz=1))
            self.l1 = wire.send(two, two, away(dz=3))
            self.give(z, 1 - y_lo)

        def forward(self, lo, left, right):
            wire.receive(right, self.rows(zl, lo), away(dz=3))
            one = self.rows(zl, lo, 0)
            to_right = wire.send(one, one, away(dz=1))
            wire.receive(left, self.rows(zr, lo), away(dz=1))
            two = self.rows(zr, lo, 1)
            to_left = wire.send(two, two, away(dz=3))
            self.give(zl, lo)
            self.give(zr, lo)
            return to_right, to_left

        def third(self):
            self.f0 = self.forward(y_lo, self.l0, self.r0)

        def fourth(self):
            self.f1 = self.forward(1 - y_lo, self.l1, self.r1)

        def last(self, lo, pair):
            wire.receive(pair[0], self.rows(zo, lo, 0), away(dz=3))
            wire.receive(pair[1], self.rows(zo, lo, 1), away(dz=1))
            self.give(zo, lo)

        def fifth(self):
            self.last(y_lo, self.f0)

        def sixth(self):
            self.last(1 - y_lo, self.f1)

        def seventh(self):
            for index, zz, lo in self.over_x:
                ref = rows_of(self.buffer, zz, lo, 80 - self.first, 80)
                wire.receive(index, ref, at((x + 3 + 2 * core) % 4, y, z, core))
                self.kept.append((wire.send(ref, ref, sibling), ref))

        def finish(self):
            for index, ref in self.kept:
                wire.receive(index, ref, sibling)

    def early(j, split):
        view = (weights, j, 1)
        return Gather(view, lambda first, count: rows_of(view, z, y_lo, first, count), split)

    out_rows, up_rows, down_rows = early(0, False), early(1, True), early(2, True)
    second_set = Gather((later_weights, 0, 3), lambda first, count: shards.at[:, ds(first, count, 16), half_cols], True)
    for load in loads[3:]:
        load.wait()
    out_rows.begin()

    def project(yh, xa):
        chip = yh * 4 + xa
        both = nt(wqkv_t[...], gathered[ds(chip * TILE, TILE, TILE), :])
        for i in range(2):
            one = both[:, i * BLK:(i + 1) * BLK]
            raw_q[2 * chip + i] = one[:HEAD_DIM]
            qkv_slot[2 * chip + i, :HEAD_DIM] = (one[:HEAD_DIM] * scale_col).astype(bf16)
            qkv_slot[2 * chip + i, HEAD_DIM:] = one[HEAD_DIM:240].astype(bf16)

    def take(indices, yh, xa, device, parts=(0, 1)):
        for part in parts:
            wire.receive(indices[part], piece(yh, xa, core, part), device)

    def to_sibling(yh, xa):
        return wire.send(piece(yh, xa, core), piece(yh, xa, core), sibling)

    def both_cores(index, yh, xa):
        wire.receive(index, piece(yh, xa, 1 - core), sibling)
        project(yh, xa)

    wire.receive(cols_y, columns_at(z, 1 - y_lo), pair)
    cols_yz = columns_round_z(1 - y_lo)
    down_rows.begin()
    up_rows.begin()
    ring, y_r, y_l = {}, {}, {}
    take(to_xr, y_hi, xl, left, (0,))
    ring[0] = pass_chunk(y_hi, xl, 0, right)
    take(to_xl, y_hi, xr, right, (1,))
    ring[1] = pass_chunk(y_hi, xr, 1, left)
    take(to_y, other, x, across, (0,))
    y_r[0] = pass_chunk(other, x, 0, right)
    y_l[0] = pass_chunk(other, x, 0, left)
    take(to_xr, y_hi, xl, left, (1,))
    core_l = to_sibling(y_hi, xl)
    take(to_xl, y_hi, xr, right, (0,))
    core_r = to_sibling(y_hi, xr)
    take(to_y, other, x, across, (1,))
    y_r[1] = pass_chunk(other, x, 1, right)
    y_l[1] = pass_chunk(other, x, 1, left)
    core_y = to_sibling(other, x)
    out_rows.begin_y()
    down_rows.begin_y()
    up_rows.begin_y()
    for index, k in zip(cols_z, (1, 3, 2)):
        wire.receive(index, columns_at((z + 4 - k) % 4, y_lo), away(dz=4 - k))
    for index, k in zip(cols_yz, (1, 3, 2)):
        wire.receive(index, columns_at((z + 4 - k) % 4, 1 - y_lo), away(dz=4 - k))
    wqkv_t[...] = flip(wqkv_all[...])
    far = {}
    wire.receive(ring[0], piece(y_hi, xo, core, 0), left)
    far[0] = pass_chunk(y_hi, xo, 0, across)
    wire.receive(ring[1], piece(y_hi, xo, core, 1), right)
    far[1] = pass_chunk(y_hi, xo, 1, across)
    core_o = to_sibling(y_hi, xo)
    out_rows.third()
    both_cores(to_core, y_hi, x)
    both_cores(core_l, y_hi, xl)
    both_cores(core_r, y_hi, xr)
    out_rows.second()
    both_cores(core_y, other, x)
    take(y_r, other, xl, left)
    core_yl = to_sibling(other, xl)
    take(y_l, other, xr, right)
    core_yr = to_sibling(other, xr)
    down_rows.second()
    up_rows.second()
    both_cores(core_o, y_hi, xo)
    down_rows.third()
    up_rows.third()
    both_cores(core_yl, other, xl)
    both_cores(core_yr, other, xr)
    take(far, other, xo, across)
    core_f = to_sibling(other, xo)
    out_rows.fourth()
    both_cores(core_f, other, xo)

    waiting = [
        down_rows.fourth, up_rows.fourth, out_rows.fifth, second_set.begin_y, second_set.begin,
        down_rows.fifth, up_rows.fifth, out_rows.sixth, down_rows.sixth, up_rows.sixth,
    ]

    def move_on(number):
        for _ in range(number):
            if waiting:
                waiting.pop(0)()

    slot_of = []
    for p in range(NBLK):
        slot = 0
        for b in range(NBLK):
            slot = jnp.where(order[0, b] == p, b, slot)
        slot_of.append(slot)
    for p in range(NBLK):
        qkv_pos[:, p * BLK:(p + 1) * BLK] = qkv_slot[slot_of[p]]
        raw_pos[:, p * BLK:(p + 1) * BLK] = raw_q[slot_of[p]]
    k_rows[...] = flip(qkv_pos[HEAD_DIM:2 * HEAD_DIM, :])
    v_rows[...] = flip(qkv_pos[2 * HEAD_DIM:, :])

    ends, total = [], 0
    for s in range(4):
        total = total + lengths[0, s]
        ends.append(total)

    at_part = 0
    parts_of = []
    for t in range(GROUP // TILE):
        low, high = max(0, t * TILE - WINDOW), (t + 1) * TILE
        width = high - low
        tile = slice(t * TILE, high)
        scores = nn(k_rows[low:high, :], qkv_pos[:HEAD_DIM, tile])
        at_q = t * TILE + lax.broadcasted_iota(jnp.int32, (1, TILE), 1)
        start = jnp.zeros((1, TILE), jnp.int32)
        for end in ends:
            start = jnp.where(at_q >= end, end, start)
        at_k = low + lax.broadcasted_iota(jnp.int32, (width, TILE), 0)
        scores = jnp.where((at_k <= at_q) & (at_k >= start), scores, MASKED)
        top = jnp.max(scores, axis=0, keepdims=True)
        powers = jnp.exp(scores - top)
        part = powers * (1.0 / jnp.sum(powers, axis=0, keepdims=True))
        part = part.astype(bf16)
        parts_of.append(slice(at_part, at_part + width))
        at_part += width
        probs[parts_of[t], :] = part
        out = nn(qkv_pos[2 * HEAD_DIM:, low:high], part).astype(bf16)
        out_pos[2 * t] = out[:, :BLK]
        out_pos[2 * t + 1] = out[:, BLK:]
        move_on(1)

    for b in range(NBLK):
        head_send[b] = out_pos[order[0, b]]

    def exchange(src_of, dst):
        return [wire.send(src_of((c + k) % 16), dst, ((c + k) % 16, f)) for k in range(1, 16)]

    def arrive(indices, dst_of):
        for k, index in enumerate(indices):
            src = (c + 15 - k) % 16
            wire.receive(index, dst_of(src), (src, f))

    head_rows = ds(c * HEAD_DIM, HEAD_DIM, HEAD_DIM)
    mixing = exchange(lambda b: head_send.at[b], mixed_t.at[head_rows])
    mixed_t[head_rows, :] = head_send[c]
    move_on(len(waiting))
    second_set.second()

    cot_f = cot[...].astype(f32)

    def spread(a, w):
        return jnp.concatenate([nn(a, weights[w, :, n:n + 256]) for n in range(0, D, 256)], axis=1)

    def spread_back(a, w):
        return jnp.concatenate([nt(a, weights[w, n:n + 256, :]) for n in range(0, D, 256)], axis=1)

    out_rows.finish()
    arrive(mixing, lambda src: mixed_t.at[ds(src * HEAD_DIM, HEAD_DIM, HEAD_DIM)])

    my_lanes, sib_lanes = ds(core * BLK, BLK, BLK), ds((1 - core) * BLK, BLK, BLK)
    other_half = ds((1 - core) * HALF, HALF, 128)

    def share(w, rows_t, up):
        acts[w, :, my_lanes] = rows_t
        up_in[w] = up
        indices = (
            wire.send(acts.at[w, :, my_lanes], acts.at[w, :, my_lanes], sibling),
            wire.send(up_in.at[w, :, other_half], up_all.at[w, my_lanes], sibling),
        )
        up_all[w, my_lanes, :] = up_in[w, :, half_cols]
        return indices

    mixed = flip(mixed_t[...])
    after = x_in + spread(mixed, 0)
    r_two = lax.rsqrt(jnp.mean(after * after, axis=1, keepdims=True) + EPS)
    n_two = after * r_two
    normed_two = (n_two * gain_two).astype(bf16)
    up_rows.seventh()
    down_rows.seventh()
    up_rows.finish()
    hidden = spread(normed_two, 1) + bias_up
    gate = jax.nn.sigmoid(hidden)
    active = (hidden * gate).astype(bf16)
    shared = {2: share(2, flip(active), cot[...])}
    down_rows.finish()
    wire.set_one = len(wire.sent)
    grad_active = spread_back(cot[...], 2)
    grad_hidden = (grad_active * gate * (1.0 + hidden * (1.0 - gate))).astype(bf16)
    shared[1] = share(1, flip(normed_two), grad_hidden)
    back_two = spread_back(grad_hidden, 1)
    scaled = back_two * gain_two
    grad_after = cot_f + r_two * (scaled - n_two * jnp.mean(scaled * n_two, axis=1, keepdims=True))
    grad_branch = grad_after.astype(bf16)
    dout_t[...] = flip(spread_back(grad_branch, 0).astype(bf16))
    douts = exchange(lambda b: dout_t.at[ds(b * HEAD_DIM, HEAD_DIM, HEAD_DIM)], dout_slot.at[c])
    dout_slot[c] = dout_t[head_rows, :]
    shared[0] = share(0, mixed_t[...], grad_branch)

    second_set.third()
    def scatter(w, stage, src_of, dst_of):
        return [wire.send(src_of((place(w, stage) + k) % 4), dst_of(k - 1), along(w, stage, k)) for k in range(1, 4)]

    def gathered_sum(w, stage, indices, first, buffers):
        for k, index in enumerate(indices):
            wire.receive(index, buffers.at[w, k], along(w, stage, 3 - k))
        return first.astype(f32) + buffers[w, 0].astype(f32) + buffers[w, 1].astype(f32) + buffers[w, 2].astype(f32)

    stage_one, stage_two, stage_three = {}, {}, {}
    for w in (2, 1, 0):
        wire.receive(shared[w][0], acts.at[w, :, sib_lanes], sibling)
        wire.receive(shared[w][1], up_all.at[w, sib_lanes], sibling)
        for n in range(0, D, 320):
            rows = slice(n, n + 320)
            t1[w, rows, :] = nn(acts[w, rows, :], up_all[w]).astype(bf16)
        stage_one[w] = scatter(w, 0, lambda d: t1.at[w, ds(d * 320, 320, 320)], lambda k: r1.at[w, k])

    layer_here[...] = (after + spread(active, 2) + bias_down).astype(bf16)
    grad_here[...] = grad_after
    put_layer = pltpu.make_async_copy(layer_here, layer_out, local_sems.at[7])
    put_layer.start()
    ar_own[...] = jnp.zeros_like(ar_own)
    ar_own[1:2, :] = jnp.sum(back_two * n_two, axis=0, keepdims=True)
    ar_own[2:3, :] = jnp.sum(grad_hidden.astype(f32), axis=0, keepdims=True)
    ar_own[3:4, :] = jnp.sum(cot_f, axis=0, keepdims=True)
    def second_stage(w):
        mine = t1[w, ds(place(w, 0) * 320, 320, 320), :]
        t2[w] = gathered_sum(w, 0, stage_one[w], mine, r1).astype(bf16)
        stage_two[w] = scatter(w, 1, lambda d: t2.at[w, ds(d * 80, 80, 80)], lambda k: r2.at[w, k])

    def third_stage(w):
        mine = t2[w, ds(place(w, 1) * 80, 80, 80), :]
        both = gathered_sum(w, 1, stage_two[w], mine, r2)
        for d in range(4):
            t3[w, d] = jnp.concatenate([both[20 * d:20 * d + 20], jnp.zeros((12, HALF), f32)], axis=0).astype(bf16)
        stage_three[w] = scatter(w, 2, lambda d: t3.at[w, d], lambda k: r3.at[w, k])

    def fourth_stage(w):
        both = gathered_sum(w, 2, stage_three[w], t3[w, place(w, 2)], r3)
        base = wire.used
        wire.used += 2
        copies = []
        for i in range(2):
            rows_out[w, i] = jnp.concatenate([both[10 * i:10 * i + 10], jnp.zeros((6, HALF), f32)], axis=0)
            target = final_target(w, i)
            stays = (target[0] == c) & (target[1] == f)
            to = rows_in.at[w, :, half_cols]
            copy = pltpu.make_async_remote_copy(
                src_ref=rows_out.at[w, i], dst_ref=to, send_sem=send_sems.at[base + i],
                recv_sem=recv_sems.at[base + core], device_id=target, device_id_type=MESH,
            )
            within = pltpu.make_async_copy(rows_out.at[w, i], to, recv_sems.at[base + core])
            pl.when(jnp.logical_not(stays))(copy.start)
            pl.when(stays)(within.start)
            copies.append((copy, stays))
        return w, base, copies

    second_set.fourth()
    arrive(douts, lambda src: dout_slot.at[src])

    for p in range(NBLK):
        dout_pos[:, p * BLK:(p + 1) * BLK] = dout_slot[slot_of[p]]
    dk_acc[...] = jnp.zeros_like(dk_acc)
    dv_acc[...] = jnp.zeros_like(dv_acc)
    scale_terms = jnp.zeros((HEAD_DIM, 1), f32)
    for t in range(GROUP // TILE):
        low, high = max(0, t * TILE - WINDOW), (t + 1) * TILE
        width = high - low
        tile = slice(t * TILE, high)
        d_out = dout_pos[:, tile]
        delta = jnp.sum(d_out.astype(f32) * jnp.concatenate([out_pos[2 * t], out_pos[2 * t + 1]], axis=1).astype(f32), axis=0, keepdims=True)
        part = probs[parts_of[t], :]
        d_probs = nn(v_rows[low:high, :], d_out)
        d_scores = (part.astype(f32) * (d_probs - delta)).astype(bf16)
        dq = nn(qkv_pos[HEAD_DIM:2 * HEAD_DIM, low:high], d_scores)
        scale_terms = scale_terms + jnp.sum(dq * raw_pos[:, tile], axis=1, keepdims=True)
        dq = (dq * scale_col).astype(bf16)
        grads_pos[2 * t, :HEAD_DIM] = dq[:, :BLK]
        grads_pos[2 * t + 1, :HEAD_DIM] = dq[:, BLK:]
        if t in (3, 6):
            (second_set.fifth, second_set.sixth)[t // 4]()
        dk_acc[:, low:high] += nt(qkv_pos[:HEAD_DIM, tile], d_scores)
        dv_acc[:, low:high] += nt(d_out, part)

    for p in range(NBLK):
        lanes = slice(p * BLK, (p + 1) * BLK)
        grads_pos[p, HEAD_DIM:2 * HEAD_DIM] = dk_acc[:, lanes].astype(bf16)
        grads_pos[p, 2 * HEAD_DIM:] = dv_acc[:, lanes].astype(bf16)
    for b in range(NBLK):
        block = grads_pos[order[0, b]]
        qkv_slot[b] = block
        grads_flat[:, b * BLK:(b + 1) * BLK] = block
    sent_grads = exchange(lambda b: qkv_slot.at[b], grads_in.at[c])
    grads_in[c] = qkv_slot[c]

    for n in range(0, D, 256):
        grad_t = nn(grads_flat[...], gathered[:, n:n + 256])
        by_gain = jnp.sum(wqkv_t[:240, n:n + 256].astype(f32) * grad_t, axis=0, keepdims=True)
        ar_own[0:1, n:n + 256] = by_gain / gain_one[:, n:n + 256]
        gw[n:n + 256, :] = jnp.concatenate([grad_t, jnp.zeros((16, 256), f32)], axis=0).T
    for fs in range(8):
        picked = [gw[cs * 80 + fs * 10:cs * 80 + fs * 10 + 10, :] for cs in range(16)]
        gw_send[fs] = jnp.concatenate(picked, axis=0).astype(bf16)
    ar_own[4:5, :HEAD_DIM] = jnp.broadcast_to(scale_terms, (HEAD_DIM, BLK)).T[:1]
    half_sums = wire.send(ar_own.at[:, other_half], ar_half, sibling)
    shares = [wire.send(gw_send.at[(f + k) % 8], gw_in.at[k - 1], (c, (f + k) % 8)) for k in range(1, 8)]

    def spread_sums(i, axis, value):
        me = here[axis]
        ar_slots[i, me] = value
        return [wire.send(ar_slots.at[i, me], ar_slots.at[i, me], away(**{"d" + axis: k})) for k in range(1, 4)]

    def collect_sums(i, axis, indices):
        for k, index in enumerate(indices):
            wire.receive(index, ar_slots.at[i, (here[axis] + 3 - k) % 4], away(**{"d" + axis: 3 - k}))
        return ar_slots[i, 0] + ar_slots[i, 1] + ar_slots[i, 2] + ar_slots[i, 3]

    wire.receive(half_sums, ar_half, sibling)
    sums = spread_sums(0, "x", ar_own[:, half_cols] + ar_half[...])
    second_set.seventh()
    second_stage(2)
    sums = spread_sums(1, "y", collect_sums(0, "x", sums))
    second_stage(1)
    second_stage(0)
    sums = spread_sums(2, "z", collect_sums(1, "y", sums))

    for k, index in enumerate(shares):
        src_f = (f + 7 - k) % 8
        wire.receive(index, gw_in.at[k], (c, src_f))
    both = gw_send[f].astype(f32)
    for k in range(7):
        both = both + gw_in[k].astype(f32)
    for cs in range(16):
        gq_send[cs] = jnp.concatenate([both[10 * cs:10 * cs + 10], jnp.zeros((6, 256), f32)], axis=0).astype(bf16)
    gq_in[c] = gq_send[c]
    heads = exchange(lambda b: gq_send.at[b], gq_in.at[c])
    third_stage(2)
    third_stage(1)
    third_stage(0)
    ar_total[:, half_cols] = collect_sums(2, "z", sums)
    half_sums = wire.send(ar_total.at[:, half_cols], ar_total.at[:, half_cols], sibling)

    second_set.finish()
    for copy in wire.sent[:wire.set_one]:
        copy.wait_send()
    wire.sent = wire.sent[wire.set_one:]
    keep.wait()
    loads = []
    for j in range(3):
        load = pltpu.make_async_copy(later_weights.at[j], weights.at[j], local_sems.at[j])
        load.start()
        loads.append(load)
    arrive(sent_grads, lambda src: grads_in.at[src])
    grad_normed = jnp.zeros((BLK, D), f32)
    for j in range(3):
        loads[j].wait()
        rows = slice(j * HEAD_DIM, (j + 1) * HEAD_DIM)
        joined = jnp.concatenate([grads_in[h, rows] for h in range(HEADS)], axis=0)
        grad_normed = grad_normed + spread_back(flip(joined), j)
    n_one = x_in * r_one
    scaled = grad_normed * gain_one
    through = r_one * (scaled - n_one * jnp.mean(scaled * n_one, axis=1, keepdims=True))
    grad_here[...] = grad_here[...] + through
    put_grad = pltpu.make_async_copy(grad_here, input_grad, local_sems.at[8])
    put_grad.start()

    finals = [fourth_stage(w) for w in (2, 1, 0)]

    wire.receive(half_sums, ar_total.at[:, other_half], sibling)
    small_out[...] = ar_total[...]
    arrive(heads, lambda src: gq_in.at[src])
    grad_qkv[...] = gq_in[...]
    for w, base, copies in finals:
        for core_at in range(2):
            wire.receive(base + core_at, rows_in.at[w, :, core_at * HALF:(core_at + 1) * HALF], final_source(w, core_at))
        for copy, stays in copies:
            pl.when(jnp.logical_not(stays))(copy.wait_send)
    grad_mlp[...] = rows_in[...]
    put_layer.wait()
    put_grad.wait()
    wire.drain()
    assert wire.used <= N_SEM


def outputs(
    out, in_grad, rows, qkv, small, q_scale,
    layer_out, input_grad, g_query, g_key, g_value, g_out, g_up, g_down, g_gain_one, g_gain_two, g_scale, g_bias_up, g_bias_down,
    layer_here, grad_here, rows_here, qkv_here, small_here, sems,
):
    places = (layer_here, grad_here, rows_here, qkv_here, small_here)
    copies = [
        pltpu.make_async_copy(src, dst, sems.at[i]) for i, (src, dst) in enumerate(zip((out, in_grad, rows, qkv, small), places))
    ]
    for copy in copies:
        copy.start()
    for copy in copies:
        copy.wait()
    stores = [
        pltpu.make_async_copy(layer_here, layer_out.at[0], sems.at[5]),
        pltpu.make_async_copy(grad_here, input_grad.at[0], sems.at[6]),
    ]
    for store in stores:
        store.start()
    rows, qkv, small = rows_here, qkv_here, small_here
    for j, ref in enumerate((g_query, g_key, g_value)):
        tiles = [jnp.zeros((16, BLK), f32) for _ in range(11)]
        for h in range(HEADS):
            tile, start = divmod(h * HEAD_DIM, BLK)
            moved = pltpu.roll(qkv[h].astype(f32), (start - j * HEAD_DIM) % 256, 1)
            lane = lax.broadcasted_iota(jnp.int32, (16, 256), 1)
            moved = jnp.where((lane >= start) & (lane < start + HEAD_DIM), moved, 0.0)
            tiles[tile] = tiles[tile] + moved[:, :BLK]
            tiles[tile + 1] = tiles[tile + 1] + moved[:, BLK:]
        ref[...] = jnp.concatenate(tiles[:10], axis=1)[:10]
    for w, ref in enumerate((g_out, g_up, g_down)):
        ref[...] = rows[w, :10, :]
    for i, ref in ((0, g_gain_one), (1, g_gain_two), (2, g_bias_up), (3, g_bias_down)):
        ref[...] = small[i, :]
    g_scale[...] = small[4, :HEAD_DIM] * QUERY_CONST * jax.nn.sigmoid(q_scale[...])
    for store in stores:
        store.wait()


def on_device(
    tokens, cotangent, lengths, block_order, w_query, w_key, w_value, w_out, w_up, w_down,
    g_attn, g_mlp, q_scale, b_up, b_down,
):
    vmem, smem, any_space = (pl.BlockSpec(memory_space=s) for s in (pltpu.VMEM, pltpu.SMEM, pl.ANY))
    shapes = {
        "weights": ((3, D, D), bf16), "shards": ((3, SHARD, D), bf16), "gathered": ((GROUP, D), bf16), "wqkv_all": ((D, 256), bf16),
        "wqkv_t": ((256, D), bf16), "raw_q": ((NBLK, HEAD_DIM, BLK), f32), "qkv_slot": ((NBLK, 240, BLK), bf16),
        "qkv_pos": ((240, GROUP), bf16), "raw_pos": ((HEAD_DIM, GROUP), f32), "k_rows": ((GROUP, HEAD_DIM), bf16),
        "v_rows": ((GROUP, HEAD_DIM), bf16), "probs": ((7680, TILE), bf16), "out_pos": ((NBLK, HEAD_DIM, BLK), bf16),
        "head_send": ((NBLK, HEAD_DIM, BLK), bf16), "mixed_t": ((D, BLK), bf16), "dout_t": ((D, BLK), bf16),
        "dout_slot": ((NBLK, HEAD_DIM, BLK), bf16), "dout_pos": ((HEAD_DIM, GROUP), bf16),
        "dk_acc": ((HEAD_DIM, GROUP), f32), "dv_acc": ((HEAD_DIM, GROUP), f32), "grads_pos": ((NBLK, 240, BLK), bf16),
        "grads_flat": ((240, GROUP), bf16), "grads_in": ((NBLK, 240, BLK), bf16),
        "acts": ((3, D, 2 * BLK), bf16), "up_in": ((3, BLK, D), bf16), "up_all": ((3, 2 * BLK, HALF), bf16),
        "t1": ((3, D, HALF), bf16), "r1": ((3, 3, 320, HALF), bf16), "t2": ((3, 320, HALF), bf16),
        "r2": ((3, 3, 80, HALF), bf16), "t3": ((3, 4, 32, HALF), bf16), "r3": ((3, 3, 32, HALF), bf16),
        "rows_out": ((3, 2, 16, HALF), f32), "rows_in": ((3, 16, D), f32),
        "gw": ((D, 256), f32), "gw_send": ((8, SHARD, 256), bf16), "gw_in": ((7, SHARD, 256), bf16),
        "gq_send": ((16, 16, 256), bf16), "gq_in": ((16, 16, 256), bf16),
        "ar_own": ((8, D), f32), "ar_half": ((8, HALF), f32), "ar_slots": ((3, 4, 8, HALF), f32),
        "ar_total": ((8, D), f32), "layer_here": ((BLK, D), bf16), "grad_here": ((BLK, D), f32),
    }
    outs = {
        "layer_out": ((BLK, D), bf16), "input_grad": ((BLK, D), f32), "grad_mlp": ((3, 16, D), f32),
        "grad_qkv": ((16, 16, 256), bf16), "small_out": ((8, D), f32), "later_weights": ((3, D, D), bf16),
    }
    ins = (
        "lengths", "order", "tokens", "cot", "w_out", "w_up", "w_down", "w_query", "w_key", "w_value",
        "g_attn", "g_mlp", "q_scale", "b_up", "b_down",
    )

    def body(*refs):
        names = ins + tuple(outs) + tuple(shapes) + ("local_sems", "send_sems", "recv_sems")
        layer(**dict(zip(names, refs, strict=True)))

    out, in_grad, rows, qkv, small, _ = pl.pallas_call(
        body,
        out_shape=[jax.ShapeDtypeStruct(*s) for s in outs.values()],
        in_specs=[smem, smem] + [vmem] * 2 + [any_space] * 6 + [vmem] * 5,
        out_specs=[any_space] * 2 + [vmem] * (len(outs) - 3) + [any_space],
        scratch_shapes=[pltpu.VMEM(*s) for s in shapes.values()]
        + [pltpu.SemaphoreType.DMA((9,)), pltpu.SemaphoreType.DMA((N_SEM,)), pltpu.SemaphoreType.DMA((N_SEM,))],
        compiler_params=pltpu.CompilerParams(
            collective_id=0, has_side_effects=True, vmem_limit_bytes=62 << 20
        ),
    )(
        lengths, block_order, tokens[0], cotangent[0], w_out, w_up, w_down, w_query, w_key, w_value,
        g_attn, g_mlp, q_scale, b_up, b_down,
    )
    row = jax.ShapeDtypeStruct((10, D), f32)
    vector = jax.ShapeDtypeStruct((D,), f32)
    return pl.pallas_call(
        outputs,
        out_shape=[
            jax.ShapeDtypeStruct((1, BLK, D), bf16), jax.ShapeDtypeStruct((1, BLK, D), f32), *[row] * 6,
            vector, vector, jax.ShapeDtypeStruct((HEAD_DIM,), f32), vector, vector,
        ],
        in_specs=[any_space] * 5 + [vmem],
        out_specs=[any_space] * 2 + [vmem] * 11,
        scratch_shapes=[
            pltpu.VMEM((BLK, D), bf16), pltpu.VMEM((BLK, D), f32),
            pltpu.VMEM((3, 16, D), f32), pltpu.VMEM((16, 16, 256), bf16), pltpu.VMEM((8, D), f32),
            pltpu.SemaphoreType.DMA((7,)),
        ],
        compiler_params=pltpu.CompilerParams(vmem_limit_bytes=62 << 20),
    )(out, in_grad, rows, qkv, small, q_scale)


def solution(mesh):
    tokens, rows, whole = P("fsdp", "ctx", None), P("fsdp", None), P()
    owned = P(("ctx", "fsdp"), None)
    return jax.shard_map(
        on_device, mesh=mesh,
        in_specs=(tokens, tokens, rows, rows) + (rows,) * 6 + (whole,) * 5,
        out_specs=(tokens, tokens) + (owned,) * 6 + (whole,) * 5,
        check_vma=False,
    )
```
